32 devices in a mesh: parts: 2 (over y), plane: 4 (over z), band: 2 (over x), sub: 2 (over core).
Axes of the slice: x: 2, y: 2, z: 4, core: 2. Of those that a mesh axis runs over, the one named last changes fastest.
Arguments:
- coefficients: float32 [2, 2, 256, 128], P(None, None, ('parts', 'plane', 'band', 'sub')), parts along dimension 2, may hold values from -6 to 6
- potential: float32 [400, 192, 192], P(('parts', 'plane', 'sub')), parts along dimension 0, may hold values from -1 to 3
- stick_column: int32 [128], replicated, may hold values from 0 to 36863, as said below
- stick_length: int32 [128], replicated, may hold values from 0 to 97, as said below
- plane_start: int32 [9], replicated, may hold values from 0 to 192, as said below
Outputs:
- applied: float32 [2, 2, 256, 128], P(None, None, ('parts', 'plane', 'band', 'sub')), parts along dimension 2
The draws below stay inside these ranges and needn't reach their ends.
There are 2 independent parts, one for each index of `parts`. The reference program is written for one: setup_inputs(seed, part) draws one part's arguments, and reference() takes and returns one part's arrays. A program takes and returns all parts, laid end to end along the dimension named above; an argument that names none is the same for every part. Nothing has to cross between parts.
Inputs may be any that keep to these rules, and one draw needn't show every extreme that they name: `stick_column`: distinct over all 128 slots; each is x * 192 + y for a column whose centred coordinates (x or x - 192, y or y - 192, the one of smaller size) lie within 48 of the anchor. `stick_length`: 0 marks an empty slot; a live stick whose column has centred coordinates (a, b) has length 2 * floor(sqrt(48^2 - a^2 - b^2)) + 1; on each device the live slots come first and number at least 4, and some device has all 8 live. `plane_start`: never falling, first entry 0, last 192; an owner holds at most 25 planes and some owner holds exactly 25.
All inputs are finite; a program needn't handle non-finite values.
Results may differ from the reference program's by a relative error of at most 0.00007.
Values sent between devices are 32-bit elements; how exact they have to be, the bound alone decides.
A program may use at most 64 MiB of HBM per device.

```python
import jax
import jax.numpy as jnp
from jax import lax

NR = 192
L = 128
SLOT_DEV = 8
OWNERS = 8
ZMAX = 25
RAD = 48
SLOTS = 128
BANDS = 2


def stick_tables(key):
    cells = NR * NR
    cell_index = jnp.arange(cells, dtype=jnp.int32)
    x_coord = cell_index // NR
    y_coord = cell_index % NR
    centre_x = jnp.where(x_coord < NR // 2, x_coord, x_coord - NR)
    centre_y = jnp.where(y_coord < NR // 2, y_coord, y_coord - NR)
    radius_sq = centre_x * centre_x + centre_y * centre_y
    inside = radius_sq <= RAD * RAD
    span_top = 2147483647 // cells - 2
    raw_score = jax.random.randint(jax.random.fold_in(key, 1), (cells,), 0, span_top)
    score = jnp.where(inside, raw_score * cells + cell_index, -1 - cell_index)
    score = score.at[0].set(2147483647).at[cells - 1].set(2147483646)
    top_values, chosen = lax.top_k(score, SLOTS)
    device_total = SLOTS // SLOT_DEV
    centre_device = jax.random.randint(jax.random.fold_in(key, 2), (), 0, device_total)
    target = centre_device * SLOT_DEV
    position = jnp.arange(SLOTS, dtype=jnp.int32)
    source = jnp.where(position == target, 0, jnp.where(position == 0, target, position))
    columns = chosen[source].astype(jnp.int32)
    live_count = jax.random.randint(jax.random.fold_in(key, 3), (device_total,), (SLOT_DEV + 1) // 2, SLOT_DEV + 1)
    full_device = jax.random.randint(jax.random.fold_in(key, 4), (), 0, device_total)
    live_count = jnp.where(jnp.arange(device_total, dtype=jnp.int32) == full_device, SLOT_DEV, live_count)
    slot_live = position % SLOT_DEV < live_count[position // SLOT_DEV]
    remain = RAD * RAD - radius_sq[columns]
    steps_range = jnp.arange(RAD + 1, dtype=jnp.int32)
    counted = jnp.sum((steps_range[None, :] * steps_range[None, :] <= remain[:, None]).astype(jnp.int32), axis=1)
    lengths = jnp.where(slot_live, 2 * counted - 1, 0).astype(jnp.int32)
    return (columns, lengths)


def draw_stick_column(key, part):
    return stick_tables(key)[0]


def draw_stick_length(key, part):
    return stick_tables(key)[1]


def draw_plane_start(key, part):
    base_count = NR // OWNERS
    remainder = NR % OWNERS
    moved = (OWNERS - remainder) // 2
    ranking = jax.random.permutation(key, OWNERS).astype(jnp.int32)
    plane_counts = base_count + (ranking < remainder + moved).astype(jnp.int32) - (ranking >= OWNERS - moved).astype(jnp.int32)
    return jnp.concatenate([jnp.zeros((1,), jnp.int32), jnp.cumsum(plane_counts).astype(jnp.int32)])


def block_levels(stream_key, extent, shards, smallest, largest):
    def one(axis_at, parts):
        steps = jax.random.uniform(jax.random.fold_in(jax.random.fold_in(stream_key, 6), axis_at), (parts,), jnp.float32, smallest / len(shards), largest / len(shards))
        return jnp.repeat(jnp.exp(steps), extent[axis_at] // parts).reshape((-1,) + (1,) * (len(extent) - axis_at - 1))

    gain = one(*shards[0])
    for cut in shards[1:]:
        gain = gain * one(*cut)
    return gain


def centred(key, extent, width, most, shards=(), held_as=jnp.bfloat16):
    gain = block_levels(key, extent, shards, -0.22, 0.18) if shards else 1.0
    array = jax.random.normal(key, extent, jnp.float32) * width * gain
    return jnp.minimum(jnp.maximum(array, -most), most).astype(held_as)


def setup_inputs(seed: int = 0, part: int = 0) -> dict:
    key_list = jax.random.split(jax.random.key(seed), 6)
    part_keys = jax.random.split(jax.random.fold_in(key_list[5], part), 6)
    coefficients = centred(part_keys[0], (2, BANDS, SLOTS, L), 1.0, 6.0, ((2, 16),), jnp.float32)
    potential = jnp.clip(-1.0 + 4.0 * jax.random.uniform(part_keys[1], (OWNERS * ZMAX, NR, NR), jnp.float32) ** block_levels(part_keys[1], (OWNERS * ZMAX, NR, NR), ((0, 8),), -0.2, 0.2), -1.0, 3.0)
    stick_column = draw_stick_column(jax.random.fold_in(key_list[5], 71), part)
    stick_length = draw_stick_length(jax.random.fold_in(key_list[5], 71), part)
    plane_start = draw_plane_start(jax.random.fold_in(key_list[5], 71), part)
    return {"coefficients": coefficients, "potential": potential, "stick_column": stick_column, "stick_length": stick_length, "plane_start": plane_start}


def reference(coefficients, potential, stick_column, stick_length, plane_start):
    slot_index = jnp.arange(L, dtype=jnp.int32)
    half_length = stick_length // 2
    live_mask = slot_index[None, :] < stick_length[:, None]
    plane_index = (slot_index[None, :] - half_length[:, None]) % NR
    grid_point = stick_column[:, None] * NR + plane_index
    plane_axis = jnp.arange(NR, dtype=jnp.int32)
    owner_of = jnp.sum((plane_start[None, 1:] <= plane_axis[:, None]).astype(jnp.int32), axis=1)
    row_index = owner_of * ZMAX + plane_axis - plane_start[owner_of]
    potential_grid = jnp.transpose(potential[row_index], (1, 2, 0))

    def one_band(band_pair):
        values = jnp.where(live_mask, band_pair[0] + 1j * band_pair[1], 0)
        psi_g = jnp.zeros(NR * NR * NR, dtype=values.dtype).at[grid_point.reshape(-1)].add(values.reshape(-1))
        psi_r = jnp.fft.ifftn(psi_g.reshape(NR, NR, NR))
        result = jnp.fft.fftn(potential_grid * psi_r).reshape(-1)[grid_point]
        return jnp.where(live_mask, result.real, 0.0), jnp.where(live_mask, result.imag, 0.0)

    real_out, imag_out = lax.map(one_band, (coefficients[0], coefficients[1]))
    return jnp.stack([real_out, imag_out]).astype(jnp.float32)
```

```python
import functools
import math

import jax
import jax.numpy as jnp
from jax import lax
from jax.experimental import pallas as pl
from jax.experimental.pallas import tpu as pltpu
from jax.sharding import PartitionSpec as P

LANES = 128
HALF = LANES // 2
SIN_TERMS = [(-1.0) ** k / math.factorial(2 * k + 1) for k in range(7)]
COS_TERMS = [(-1.0) ** k / math.factorial(2 * k) for k in range(8)]


def series(square, terms):
    total = jnp.full_like(square, terms[-1])
    for term in reversed(terms[:-1]):
        total = total * square + term
    return total


def phases(product, grid_size):
    turns = product * (1.0 / grid_size)
    rest = product - grid_size * jnp.floor(turns + 0.5)
    angle = rest * (math.pi / grid_size)
    square = angle * angle
    half_sin = angle * series(square, SIN_TERMS)
    half_cos = series(square, COS_TERMS)
    return 1.0 - 2.0 * half_sin * half_sin, 2.0 * half_sin * half_cos


def split(values):
    high = values.astype(jnp.bfloat16)
    low = (values - high.astype(jnp.float32)).astype(jnp.bfloat16)
    return high, low


def dot(left, right):
    return jnp.dot(left, right, preferred_element_type=jnp.float32)


def dot_rows(left, right):
    return lax.dot_general(
        left, right, (((1,), (1,)), ((), ())), preferred_element_type=jnp.float32
    )


def rows_of(shape):
    return lax.broadcasted_iota(jnp.int32, shape, 0)


def lanes_of(shape):
    return lax.broadcasted_iota(jnp.int32, shape, 1)


def whole(values, divisor):
    return jnp.floor((values + 0.5) * (1.0 / divisor))


def fused_kernel(
    sizes,
    start_smem,
    length_smem,
    column_row,
    length_row,
    coef_ref,
    pot_hbm,
    out_ref,
    line_high,
    line_low,
    send_buf,
    recv_buf,
    ret_buf,
    back_buf,
    pot_vmem,
    combined,
    x_cos,
    x_sin,
    y_up,
    y_down,
    values,
    result,
    pot_sem,
    send_sem,
    recv_sem,
    send_back_sem,
    recv_back_sem,
):
    plane_count, band_count, sub_count, owners, depth, grid, slots, dev_slots, coef_slots, block = sizes
    span = -(-depth // 16) * 16
    devices = plane_count * band_count * sub_count
    half_grid = grid // 2
    wide = y_down.shape[0] // 2

    part = lax.axis_index("parts")
    plane_pos = lax.axis_index("plane")
    band_pos = lax.axis_index("band")
    sub_pos = lax.axis_index("sub")
    me = (plane_pos * band_count + band_pos) * sub_count + sub_pos
    my_owner = plane_pos * sub_count + sub_pos

    def place(step):
        other = lax.rem(me + step, devices)
        other_sub = lax.rem(other, sub_count)
        other_band = lax.rem(other // sub_count, band_count)
        other_plane = other // (sub_count * band_count)
        owner = other_plane * sub_count + other_sub
        return other, owner, other_band, (part, other_plane, other_band, other_sub)

    barrier = pltpu.get_barrier_semaphore()
    for step in range(1, devices):
        pl.semaphore_signal(
            barrier, inc=1, device_id=place(step)[3], device_id_type=pl.DeviceIdType.MESH
        )
    pot_copy = pltpu.make_async_copy(pot_hbm, pot_vmem, pot_sem)
    pot_copy.start()

    def line_block(owner, carry):
        first = start_smem[owner]
        count = start_smem[owner + 1] - first
        shape = (span, coef_slots)
        row = rows_of(shape)
        product = (row + first).astype(jnp.float32) * lanes_of(shape).astype(jnp.float32)
        cos, sin = phases(product, float(grid))
        held = row < count
        cos = jnp.where(held, cos, 0.0)
        sin = jnp.where(held, sin, 0.0)
        blank = jnp.zeros((HALF - span, 2 * coef_slots), jnp.float32)
        rows = jnp.concatenate(
            [
                jnp.concatenate([cos, -sin], axis=1),
                blank,
                jnp.concatenate([sin, cos], axis=1),
                blank,
            ],
            axis=0,
        )
        high, low = split(rows)
        at = pl.ds(pl.multiple_of(owner * LANES, LANES), LANES)
        line_high[at, :] = high
        line_low[at, :] = low
        return carry

    lax.fori_loop(0, owners, line_block, 0, unroll=True)

    lane_small = lanes_of((dev_slots, coef_slots))
    row_small = rows_of((dev_slots, coef_slots))
    own_length = jnp.zeros((dev_slots, coef_slots), jnp.int32)
    for slot in range(dev_slots):
        own_length = jnp.where(row_small == slot, length_smem[me * dev_slots + slot], own_length)
    live = lane_small < own_length
    held = jnp.concatenate(
        [
            jnp.concatenate(
                [jnp.where(live, coef_ref[0, b], 0.0), jnp.where(live, coef_ref[1, b], 0.0)], axis=1
            )
            for b in range(band_count)
        ],
        axis=0,
    )
    high, low = split(held)
    both = dot_rows(jnp.concatenate([high, low], axis=0), line_high[...])
    rows = band_count * dev_slots
    sent = both[:rows] + both[rows:] + dot_rows(high, line_low[...])
    for owner in range(owners):
        for b in range(band_count):
            send_buf[owner, b] = sent[
                b * dev_slots : (b + 1) * dev_slots, owner * LANES : (owner + 1) * LANES
            ]

    pl.semaphore_wait(barrier, devices - 1)

    my_rows = pl.ds(pl.multiple_of(me * dev_slots, dev_slots), dev_slots)

    def outward(step):
        other, owner, band, device = place(step)
        return pltpu.make_async_remote_copy(
            src_ref=send_buf.at[owner, band],
            dst_ref=recv_buf.at[my_rows],
            send_sem=send_sem.at[step - 1],
            recv_sem=recv_sem.at[step - 1],
            device_id=device,
            device_id_type=pl.DeviceIdType.MESH,
        )

    def homeward(step):
        other, owner, band, device = place(step)
        return pltpu.make_async_remote_copy(
            src_ref=ret_buf.at[pl.ds(pl.multiple_of(other * dev_slots, dev_slots), dev_slots)],
            dst_ref=back_buf.at[my_owner, band_pos],
            send_sem=send_back_sem.at[step - 1],
            recv_sem=recv_back_sem.at[step - 1],
            device_id=device,
            device_id_type=pl.DeviceIdType.MESH,
        )

    for step in range(1, devices):
        outward(step).start()
    recv_buf[my_rows, :] = send_buf[my_owner, band_pos]

    column = column_row[...].astype(jnp.float32)
    column_x = whole(column, grid)
    column_y = column - grid * column_x
    cos, sin = phases(rows_of((grid, slots)).astype(jnp.float32) * column_x, float(grid))
    x_cos[...] = cos
    x_sin[...] = sin
    cos, sin = phases(rows_of((wide, slots)).astype(jnp.float32) * column_y, float(grid))
    high, low = split(jnp.concatenate([cos, sin], axis=0))
    y_down[:, :slots] = high
    y_down[:, slots:] = low
    high, low = split(jnp.concatenate([cos.T, sin.T], axis=1))
    y_up[:slots] = high
    y_up[slots : 2 * slots] = high
    y_up[2 * slots :] = low
    half_length = whole(length_row[...].astype(jnp.float32), 2)
    my_first = start_smem[my_owner]
    turn_cos, turn_sin = phases(
        (rows_of((span, slots)) + my_first).astype(jnp.float32) * half_length, float(grid)
    )

    row = rows_of((grid, wide))
    lane = lanes_of((grid, wide))
    same = jnp.where((row == lane) & (lane <= half_grid), 1.0, 0.0)
    mirror = jnp.where((row + lane == grid) & (lane < half_grid), 1.0, 0.0)
    inner = jnp.where((row == lane) & (lane < half_grid) & (lane > 0), 1.0, 0.0)
    pairing = jnp.concatenate([same + mirror, inner - mirror], axis=1).astype(jnp.bfloat16)
    pot_copy.wait()

    def combine(step, carry):
        for i in range(block):
            z = step * block + i
            high, low = split(pot_vmem[z])
            combined[z] = dot(high, pairing) + dot(low, pairing)
        return carry

    lax.fori_loop(0, depth // block, combine, 0)
    result[...] = jnp.zeros_like(result)

    for step in range(1, devices):
        outward(step).wait_recv()
    turned = recv_buf[...].T
    got_real = turned[:span]
    got_imag = turned[HALF : HALF + span]
    values[0] = got_real * turn_cos + got_imag * turn_sin
    values[1] = got_imag * turn_cos - got_real * turn_sin

    def planes(step, carry):
        for i in range(block):
            z = step * block + i
            real = values[0, pl.ds(z, 1), :]
            imag = values[1, pl.ds(z, 1), :]
            ax = x_cos[...]
            bx = x_sin[...]
            high, low = split(
                jnp.concatenate([ax * real - bx * imag, ax * imag + bx * real], axis=0)
            )
            psi = dot(jnp.concatenate([high, low, high], axis=1), y_up[...])
            even_real, odd_real = psi[:grid, :wide], psi[:grid, wide:]
            even_imag, odd_imag = psi[grid:, :wide], psi[grid:, wide:]
            even = combined[z, :, :wide]
            odd = combined[z, :, wide:]
            product = jnp.concatenate(
                [
                    jnp.concatenate(
                        [
                            even * even_real - odd * odd_imag,
                            odd * even_imag + even * odd_real,
                        ],
                        axis=1,
                    ),
                    jnp.concatenate(
                        [
                            even * even_imag + odd * odd_real,
                            even * odd_imag - odd * even_real,
                        ],
                        axis=1,
                    ),
                ],
                axis=0,
            )
            high, low = split(product)
            first = dot(high, y_down[...])
            back = first[:, :slots] + first[:, slots:] + dot(low, y_down[:, :slots])
            back_real, back_imag = back[:grid], back[grid:]
            result[pl.ds(z, 1), :] = jnp.sum(ax * back_real + bx * back_imag, axis=0, keepdims=True)
            result[pl.ds(HALF + z, 1), :] = jnp.sum(
                ax * back_imag - bx * back_real, axis=0, keepdims=True
            )
        return carry

    lax.fori_loop(0, depth // block, planes, 0)

    out_real = result[:span]
    out_imag = result[HALF : HALF + span]
    blank = jnp.zeros((HALF - span, slots), jnp.float32)
    ret_buf[...] = jnp.concatenate(
        [
            out_real * turn_cos - out_imag * turn_sin,
            blank,
            out_imag * turn_cos + out_real * turn_sin,
            blank,
        ],
        axis=0,
    ).T
    for step in range(1, devices):
        homeward(step).start()
    back_buf[my_owner, band_pos] = ret_buf[my_rows, :]
    for step in range(1, devices):
        homeward(step).wait_recv()

    lines = jnp.concatenate(
        [
            jnp.concatenate([back_buf[owner, b] for b in range(band_count)], axis=0)
            for owner in range(owners)
        ],
        axis=1,
    )
    high, low = split(lines)
    both = dot(jnp.concatenate([high, low], axis=0), line_high[...])
    applied = both[:rows] + both[rows:] + dot(high, line_low[...])
    applied = applied * (1.0 / float(grid * grid * grid))
    for b in range(band_count):
        for c in range(2):
            piece = applied[
                b * dev_slots : (b + 1) * dev_slots, c * coef_slots : (c + 1) * coef_slots
            ]
            out_ref[c, b] = jnp.where(live, piece, 0.0)

    for step in range(1, devices):
        outward(step).wait_send()
        homeward(step).wait_send()


def on_device_fused(coefficients, potential, stick_column, stick_length, plane_start):
    plane_count = lax.axis_size("plane")
    band_count = lax.axis_size("band")
    sub_count = lax.axis_size("sub")
    owners = plane_count * sub_count
    depth, grid = potential.shape[0], potential.shape[1]
    dev_slots, coef_slots = coefficients.shape[2], coefficients.shape[3]
    slots = stick_column.shape[0]
    devices = plane_count * band_count * sub_count
    wide = -(-(grid // 2 + 1) // LANES) * LANES
    span = -(-depth // 16) * 16
    block = max(k for k in range(1, 6) if depth % k == 0)
    sizes = (
        plane_count, band_count, sub_count, owners, depth, grid, slots, dev_slots, coef_slots, block
    )
    f32, bf16 = jnp.float32, jnp.bfloat16
    vmem = pl.BlockSpec(memory_space=pltpu.VMEM)
    smem = pl.BlockSpec(memory_space=pltpu.SMEM)
    return pl.pallas_call(
        functools.partial(fused_kernel, sizes),
        out_shape=jax.ShapeDtypeStruct(coefficients.shape, f32),
        in_specs=[smem, smem, vmem, vmem, vmem, pl.BlockSpec(memory_space=pl.ANY)],
        out_specs=vmem,
        scratch_shapes=[
            pltpu.VMEM((owners * LANES, 2 * coef_slots), bf16),
            pltpu.VMEM((owners * LANES, 2 * coef_slots), bf16),
            pltpu.VMEM((owners, band_count, dev_slots, LANES), f32),
            pltpu.VMEM((slots, LANES), f32),
            pltpu.VMEM((slots, LANES), f32),
            pltpu.VMEM((owners, band_count, dev_slots, LANES), f32),
            pltpu.VMEM(potential.shape, f32),
            pltpu.VMEM((depth, grid, 2 * wide), f32),
            pltpu.VMEM((grid, slots), f32),
            pltpu.VMEM((grid, slots), f32),
            pltpu.VMEM((3 * slots, 2 * wide), bf16),
            pltpu.VMEM((2 * wide, 2 * slots), bf16),
            pltpu.VMEM((2, span, slots), f32),
            pltpu.VMEM((LANES, slots), f32),
            pltpu.SemaphoreType.DMA,
            pltpu.SemaphoreType.DMA((devices - 1,)),
            pltpu.SemaphoreType.DMA((devices - 1,)),
            pltpu.SemaphoreType.DMA((devices - 1,)),
            pltpu.SemaphoreType.DMA((devices - 1,)),
        ],
        compiler_params=pltpu.CompilerParams(
            collective_id=0, has_side_effects=True, vmem_limit_bytes=48 * 1024 * 1024
        ),
        cost_estimate=pl.CostEstimate(
            flops=4 * depth * 2 * grid * slots * 2 * wide,
            bytes_accessed=potential.size * 4,
            transcendentals=0,
        ),
    )(
        plane_start,
        stick_length,
        stick_column.reshape(1, slots),
        stick_length.reshape(1, slots),
        coefficients,
        potential,
    )


two_pi = 2.0 * math.pi
precise = lax.Precision.HIGHEST


def phase_table(product, grid_size):
    angle = (product % grid_size).astype(jnp.float32) * (two_pi / grid_size)
    return (jnp.cos(angle), jnp.sin(angle))


def global_slot(owner_src, band_src, within, band_count, sub_count, dev_slots):
    return (
        (owner_src // sub_count * band_count + band_src) * sub_count + owner_src % sub_count
    ) * dev_slots + within


def inverse_columns(parts, lengths, line_cos, line_sin, plane_z, grid_size):
    live_mask = jnp.arange(parts.shape[3], dtype=jnp.int32)[None, :] < lengths[:, None]
    real_part = jnp.where(live_mask, parts[0], 0.0)
    imag_part = jnp.where(live_mask, parts[1], 0.0)
    first_real = jnp.einsum("bsl,lq->bqs", real_part, line_cos, precision=precise) - jnp.einsum(
        "bsl,lq->bqs", imag_part, line_sin, precision=precise
    )
    first_imag = jnp.einsum("bsl,lq->bqs", real_part, line_sin, precision=precise) + jnp.einsum(
        "bsl,lq->bqs", imag_part, line_cos, precision=precise
    )
    shift_cos, shift_sin = phase_table(plane_z[:, None] * (lengths // 2)[None, :], grid_size)
    out_real = first_real * shift_cos + first_imag * shift_sin
    out_imag = first_imag * shift_cos - first_real * shift_sin
    return jnp.stack([out_real, out_imag])


def forward_columns(data, lengths, line_cos, line_sin, plane_z, grid_size):
    shift_cos, shift_sin = phase_table(plane_z[:, None] * (lengths // 2)[None, :], grid_size)
    turn_real = data[0] * shift_cos - data[1] * shift_sin
    turn_imag = data[1] * shift_cos + data[0] * shift_sin
    out_real = jnp.einsum("bqs,lq->bsl", turn_real, line_cos, precision=precise) + jnp.einsum(
        "bqs,lq->bsl", turn_imag, line_sin, precision=precise
    )
    out_imag = jnp.einsum("bqs,lq->bsl", turn_imag, line_cos, precision=precise) - jnp.einsum(
        "bqs,lq->bsl", turn_real, line_sin, precision=precise
    )
    scale = 1.0 / float(grid_size * grid_size * grid_size)
    live_mask = jnp.arange(line_cos.shape[0], dtype=jnp.int32)[None, :] < lengths[:, None]
    return jnp.stack(
        [jnp.where(live_mask, out_real * scale, 0.0), jnp.where(live_mask, out_imag * scale, 0.0)]
    )


def complex_table(dft_cos, dft_sin, sign):
    from_real = jnp.stack([dft_cos, sign * dft_sin], axis=1)
    from_imag = jnp.stack([-sign * dft_sin, dft_cos], axis=1)
    return jnp.stack([from_real, from_imag])


def apply_planes(received, columns, potential, grid_size):
    depth_count = received.shape[1]
    radius = grid_size // 4
    compact = 2 * radius + 1
    col_x = columns // grid_size
    col_y = columns % grid_size
    small_x = jnp.where(col_x <= radius, col_x, col_x - grid_size + compact)
    small_y = jnp.where(col_y <= radius, col_y, col_y - grid_size + compact)
    small_index = small_x * compact + small_y
    spread = (
        jnp.zeros((2, depth_count, compact * compact), jnp.float32)
        .at[:, :, small_index]
        .add(received)
    )
    spread = jnp.transpose(spread.reshape(2, depth_count, compact, compact), (1, 2, 0, 3))
    small_axis = jnp.arange(compact, dtype=jnp.int32)
    wave_freq = jnp.where(small_axis <= radius, small_axis, small_axis - compact + grid_size)
    wave_index = jnp.arange(grid_size, dtype=jnp.int32)
    up_cos, up_sin = phase_table(wave_freq[:, None] * wave_index[None, :], grid_size)
    down_cos, down_sin = phase_table(wave_index[:, None] * wave_freq[None, :], grid_size)
    table_plus = complex_table(up_cos, up_sin, 1.0)
    table_minus = complex_table(down_cos, down_sin, -1.0)
    spread = jnp.einsum("zacb,cadx->zxdb", spread, table_plus, precision=precise)
    spread = jnp.einsum("zxcb,cbdk->zxdk", spread, table_plus, precision=precise)
    spread = spread * potential[:, :, None, :]
    spread = jnp.einsum("zxcy,cydk->zxdk", spread, table_minus, precision=precise)
    spread = jnp.einsum("zxcb,cxda->zadb", spread, table_minus, precision=precise)
    planes_flat = jnp.transpose(spread, (2, 0, 1, 3)).reshape(2, depth_count, compact * compact)
    return planes_flat[:, :, small_index]


def on_device(coefficients, potential, stick_column, stick_length, plane_start):
    plane_count = lax.axis_size("plane")
    band_count = lax.axis_size("band")
    sub_count = lax.axis_size("sub")
    owners_count = plane_count * sub_count
    plane_depth = potential.shape[0]
    grid_size = potential.shape[1]
    coef_slots = coefficients.shape[3]
    dev_slots = coefficients.shape[2]
    group_slots = band_count * dev_slots
    plane_pos = lax.axis_index("plane")
    sub_pos = lax.axis_index("sub")
    my_owner = plane_pos * sub_count + sub_pos
    plane_counts = plane_start[1:] - plane_start[:-1]
    depth_index = jnp.arange(plane_depth, dtype=jnp.int32)
    valid_plane = (depth_index[None, :] < plane_counts[:, None]).reshape(-1)
    plane_z = jnp.where(
        valid_plane, (plane_start[:-1][:, None] + depth_index[None, :]).reshape(-1), 0
    )
    line_index = jnp.arange(coef_slots, dtype=jnp.int32)
    line_cos, line_sin = phase_table(line_index[:, None] * plane_z[None, :], grid_size)
    valid_float = valid_plane.astype(jnp.float32)[None, :]
    line_cos = line_cos * valid_float
    line_sin = line_sin * valid_float
    owner_axis = jnp.arange(owners_count, dtype=jnp.int32)
    band_axis = jnp.arange(band_count, dtype=jnp.int32)
    within_axis = jnp.arange(dev_slots, dtype=jnp.int32)
    owner_major = global_slot(
        owner_axis[:, None, None],
        band_axis[None, :, None],
        within_axis[None, None, :],
        band_count,
        sub_count,
        dev_slots,
    ).reshape(-1)
    total_slots = owner_major.shape[0]
    question = plane_depth * owners_count
    group_ids = global_slot(
        my_owner, band_axis[:, None], within_axis[None, :], band_count, sub_count, dev_slots
    ).reshape(-1)
    group_len = stick_length[group_ids]
    regrouped = lax.all_to_all(coefficients, "band", split_axis=1, concat_axis=2, tiled=True)
    columns_z = inverse_columns(regrouped, group_len, line_cos, line_sin, plane_z, grid_size)
    columns_z = columns_z.reshape(2, 1, owners_count, plane_depth, group_slots)
    arrived = lax.all_to_all(columns_z, ("plane", "sub"), split_axis=2, concat_axis=4, tiled=True)
    planes_out = apply_planes(
        arrived.reshape(2, plane_depth, total_slots),
        stick_column[owner_major],
        potential,
        grid_size,
    )
    returned = lax.all_to_all(
        planes_out.reshape(2, 1, 1, plane_depth, total_slots),
        ("plane", "sub"),
        split_axis=4,
        concat_axis=2,
        tiled=True,
    )
    coef_back = forward_columns(
        returned.reshape(2, 1, question, group_slots),
        group_len,
        line_cos,
        line_sin,
        plane_z,
        grid_size,
    )
    applied = lax.all_to_all(coef_back, "band", split_axis=2, concat_axis=1, tiled=True)
    return applied


def on_device_any(coefficients, potential, stick_column, stick_length, plane_start):
    small = (
        stick_column.shape[0] <= 512 and potential.shape[0] <= HALF and coefficients.shape[2] == 8
    )
    chosen = on_device_fused if small else on_device
    return chosen(coefficients, potential, stick_column, stick_length, plane_start)


def solution(mesh):
    placed = (
        P(None, None, ("parts", "plane", "band", "sub"), None),
        P(("parts", "plane", "sub"), None, None),
        P(),
        P(),
        P(),
    )
    return jax.shard_map(
        on_device_any,
        mesh=mesh,
        in_specs=placed,
        out_specs=P(None, None, ("parts", "plane", "band", "sub"), None),
        check_vma=False,
    )
```

```python
import functools
import math

import jax
import jax.numpy as jnp
from jax import lax
from jax.experimental import pallas as pl
from jax.experimental.pallas import tpu as pltpu
from jax.sharding import PartitionSpec as P

LANES = 128
HALF = LANES // 2
SIN_TERMS = [(-1.0) ** k / math.factorial(2 * k + 1) for k in range(7)]
COS_TERMS = [(-1.0) ** k / math.factorial(2 * k) for k in range(8)]


def series(square, terms):
    total = jnp.full_like(square, terms[-1])
    for term in reversed(terms[:-1]):
        total = total * square + term
    return total


def phases(product, grid_size):
    turns = product * (1.0 / grid_size)
    rest = product - grid_size * jnp.floor(turns + 0.5)
    angle = rest * (math.pi / grid_size)
    square = angle * angle
    half_sin = angle * series(square, SIN_TERMS)
    half_cos = series(square, COS_TERMS)
    return 1.0 - 2.0 * half_sin * half_sin, 2.0 * half_sin * half_cos


def split(values):
    high = values.astype(jnp.bfloat16)
    low = (values - high.astype(jnp.float32)).astype(jnp.bfloat16)
    return high, low


def dot(left, right):
    return jnp.dot(left, right, preferred_element_type=jnp.float32)


def dot_rows(left, right):
    return lax.dot_general(
        left, right, (((1,), (1,)), ((), ())), preferred_element_type=jnp.float32
    )


def rows_of(shape):
    return lax.broadcasted_iota(jnp.int32, shape, 0)


def lanes_of(shape):
    return lax.broadcasted_iota(jnp.int32, shape, 1)


def whole(values, divisor):
    return jnp.floor((values + 0.5) * (1.0 / divisor))


def fused_kernel(
    sizes,
    start_hbm,
    length_hbm,
    column_row_hbm,
    length_row_hbm,
    coef_hbm,
    pot_hbm,
    out_ref,
    start_smem,
    length_smem,
    column_row,
    length_row,
    coef_ref,
    line_high,
    line_low,
    send_buf,
    recv_buf,
    ret_buf,
    back_buf,
    pot_vmem,
    combined,
    x_cos,
    x_sin,
    y_up,
    y_down,
    values,
    result,
    pot_sem,
    small_sem,
    out_sems,
    home_sems,
):
    plane_count, band_count, sub_count, owners, depth, grid, slots, dev_slots, coef_slots, block = sizes
    span = -(-depth // 16) * 16
    devices = plane_count * band_count * sub_count
    half_grid = grid // 2
    wide = y_down.shape[0] // 2

    part = lax.axis_index("parts")
    plane_pos = lax.axis_index("plane")
    band_pos = lax.axis_index("band")
    sub_pos = lax.axis_index("sub")
    me = (plane_pos * band_count + band_pos) * sub_count + sub_pos
    my_owner = plane_pos * sub_count + sub_pos

    def wrap(position, offset, count):
        moved = position + offset
        return jnp.where(moved >= count, moved - count, moved)

    def place(step):
        other_plane = wrap(plane_pos, step[0], plane_count)
        other_band = wrap(band_pos, step[1], band_count)
        other_sub = wrap(sub_pos, step[2], sub_count)
        owner = other_plane * sub_count + other_sub
        other = (other_plane * band_count + other_band) * sub_count + other_sub
        tile = owner * band_count + other_band
        return other, tile, (part, other_plane, other_band, other_sub)

    steps = [
        (p, b, s)
        for p in sorted(range(plane_count), key=lambda p: -min(p, plane_count - p))
        for b in reversed(range(band_count))
        for s in reversed(range(sub_count))
        if p + b + s > 0
    ]
    places = [place(step) for step in steps]
    my_tile = my_owner * band_count + band_pos

    small_copies = [
        pltpu.make_async_copy(source, target, small_sem.at[i])
        for i, (source, target) in enumerate(
            [
                (start_hbm, start_smem),
                (length_hbm, length_smem),
                (coef_hbm, coef_ref),
                (column_row_hbm, column_row),
                (length_row_hbm, length_row),
            ]
        )
    ]
    for copy in small_copies:
        copy.start()
    barrier = pltpu.get_barrier_semaphore()
    for _, _, device in places:
        pl.semaphore_signal(
            barrier, inc=1, device_id=device, device_id_type=pl.DeviceIdType.MESH
        )
    pot_copy = pltpu.make_async_copy(pot_hbm, pot_vmem, pot_sem)
    pot_copy.start()

    for copy in small_copies:
        copy.wait()

    def line_block(owner, carry):
        first = start_smem[owner]
        count = start_smem[owner + 1] - first
        shape = (span, coef_slots)
        row = rows_of(shape)
        product = (row + first).astype(jnp.float32) * lanes_of(shape).astype(jnp.float32)
        cos, sin = phases(product, float(grid))
        held = row < count
        cos = jnp.where(held, cos, 0.0)
        sin = jnp.where(held, sin, 0.0)
        blank = jnp.zeros((HALF - span, 2 * coef_slots), jnp.float32)
        rows = jnp.concatenate(
            [
                jnp.concatenate([cos, -sin], axis=1),
                blank,
                jnp.concatenate([sin, cos], axis=1),
                blank,
            ],
            axis=0,
        )
        high, low = split(rows)
        at = pl.ds(pl.multiple_of(owner * LANES, LANES), LANES)
        line_high[at, :] = high
        line_low[at, :] = low
        return carry

    lax.fori_loop(0, owners, line_block, 0, unroll=True)

    lane_small = lanes_of((dev_slots, coef_slots))
    row_small = rows_of((dev_slots, coef_slots))
    own_length = jnp.zeros((dev_slots, coef_slots), jnp.int32)
    for slot in range(dev_slots):
        own_length = jnp.where(row_small == slot, length_smem[me * dev_slots + slot], own_length)
    live = lane_small < own_length
    held = jnp.concatenate(
        [
            jnp.concatenate(
                [jnp.where(live, coef_ref[0, b], 0.0), jnp.where(live, coef_ref[1, b], 0.0)], axis=1
            )
            for b in range(band_count)
        ],
        axis=0,
    )
    high, low = split(held)
    both = dot_rows(jnp.concatenate([high, low], axis=0), line_high[...])
    rows = band_count * dev_slots
    sent = both[:rows] + both[rows:] + dot_rows(high, line_low[...])
    for owner in range(owners):
        for b in range(band_count):
            send_buf[owner * band_count + b] = sent[
                b * dev_slots : (b + 1) * dev_slots, owner * LANES : (owner + 1) * LANES
            ]

    pl.semaphore_wait(barrier, devices - 1)

    def send(source, target, sems, device):
        return pltpu.make_async_remote_copy(
            src_ref=source,
            dst_ref=target,
            send_sem=sems.at[0],
            recv_sem=sems.at[1],
            device_id=device,
            device_id_type=pl.DeviceIdType.MESH,
        )

    def all_of(buffer, sems):
        others = buffer.at[pl.ds(0, devices - 1)]
        return send(others, others, sems, places[0][2])

    for _, tile, device in places:
        send(send_buf.at[tile], recv_buf.at[me], out_sems, device).start()
    recv_buf[me] = send_buf[my_tile]

    column = column_row[...].astype(jnp.float32)
    column_x = whole(column, grid)
    column_y = column - grid * column_x
    cos, sin = phases(rows_of((grid, slots)).astype(jnp.float32) * column_x, float(grid))
    x_cos[...] = cos
    x_sin[...] = sin
    cos, sin = phases(rows_of((wide, slots)).astype(jnp.float32) * column_y, float(grid))
    high, low = split(jnp.concatenate([cos, sin], axis=0))
    y_down[:, :slots] = high
    y_down[:, slots:] = low
    high, low = split(jnp.concatenate([cos.T, sin.T], axis=1))
    y_up[:slots] = high
    y_up[slots : 2 * slots] = high
    y_up[2 * slots :] = low
    half_length = whole(length_row[...].astype(jnp.float32), 2)
    my_first = start_smem[my_owner]
    turn_cos, turn_sin = phases(
        (rows_of((span, slots)) + my_first).astype(jnp.float32) * half_length, float(grid)
    )

    row = rows_of((grid, wide))
    lane = lanes_of((grid, wide))
    same = jnp.where((row == lane) & (lane <= half_grid), 1.0, 0.0)
    mirror = jnp.where((row + lane == grid) & (lane < half_grid), 1.0, 0.0)
    inner = jnp.where((row == lane) & (lane < half_grid) & (lane > 0), 1.0, 0.0)
    pairing = jnp.concatenate([same + mirror, inner - mirror], axis=1).astype(jnp.bfloat16)
    pot_copy.wait()

    def combine(step, carry):
        for i in range(block):
            z = step * block + i
            high, low = split(pot_vmem[z])
            combined[z] = dot(high, pairing) + dot(low, pairing)
        return carry

    lax.fori_loop(0, depth // block, combine, 0)
    result[...] = jnp.zeros_like(result)

    all_of(recv_buf, out_sems).wait_recv()
    turned = recv_buf[...].reshape(slots, LANES).T
    got_real = turned[:span]
    got_imag = turned[HALF : HALF + span]
    values[0] = got_real * turn_cos + got_imag * turn_sin
    values[1] = got_imag * turn_cos - got_real * turn_sin

    def planes(step, carry):
        for i in range(block):
            z = step * block + i
            real = values[0, pl.ds(z, 1), :]
            imag = values[1, pl.ds(z, 1), :]
            ax = x_cos[...]
            bx = x_sin[...]
            high, low = split(
                jnp.concatenate([ax * real - bx * imag, ax * imag + bx * real], axis=0)
            )
            psi = dot(jnp.concatenate([high, low, high], axis=1), y_up[...])
            even_real, odd_real = psi[:grid, :wide], psi[:grid, wide:]
            even_imag, odd_imag = psi[grid:, :wide], psi[grid:, wide:]
            even = combined[z, :, :wide]
            odd = combined[z, :, wide:]
            product = jnp.concatenate(
                [
                    jnp.concatenate(
                        [
                            even * even_real - odd * odd_imag,
                            odd * even_imag + even * odd_real,
                        ],
                        axis=1,
                    ),
                    jnp.concatenate(
                        [
                            even * even_imag + odd * odd_real,
                            even * odd_imag - odd * even_real,
                        ],
                        axis=1,
                    ),
                ],
                axis=0,
            )
            high, low = split(product)
            first = dot(high, y_down[...])
            back = first[:, :slots] + first[:, slots:] + dot(low, y_down[:, :slots])
            back_real, back_imag = back[:grid], back[grid:]
            result[pl.ds(z, 1), :] = jnp.sum(ax * back_real + bx * back_imag, axis=0, keepdims=True)
            result[pl.ds(HALF + z, 1), :] = jnp.sum(
                ax * back_imag - bx * back_real, axis=0, keepdims=True
            )
        return carry

    lax.fori_loop(0, depth // block, planes, 0)

    out_real = result[:span]
    out_imag = result[HALF : HALF + span]
    blank = jnp.zeros((HALF - span, slots), jnp.float32)
    ret_buf[...] = jnp.concatenate(
        [
            out_real * turn_cos - out_imag * turn_sin,
            blank,
            out_imag * turn_cos + out_real * turn_sin,
            blank,
        ],
        axis=0,
    ).T.reshape(devices, dev_slots, LANES)
    for other, _, device in places:
        send(ret_buf.at[other], back_buf.at[my_tile], home_sems, device).start()
    back_buf[my_tile] = ret_buf[me]
    all_of(back_buf, home_sems).wait_recv()

    lines = jnp.concatenate(
        [
            jnp.concatenate([back_buf[owner * band_count + b] for b in range(band_count)], axis=0)
            for owner in range(owners)
        ],
        axis=1,
    )
    high, low = split(lines)
    both = dot(jnp.concatenate([high, low], axis=0), line_high[...])
    applied = both[:rows] + both[rows:] + dot(high, line_low[...])
    applied = applied * (1.0 / float(grid * grid * grid))
    for b in range(band_count):
        for c in range(2):
            piece = applied[
                b * dev_slots : (b + 1) * dev_slots, c * coef_slots : (c + 1) * coef_slots
            ]
            out_ref[c, b] = jnp.where(live, piece, 0.0)

    all_of(send_buf, out_sems).wait_send()
    all_of(ret_buf, home_sems).wait_send()


def on_device_fused(coefficients, potential, stick_column, stick_length, plane_start):
    plane_count = lax.axis_size("plane")
    band_count = lax.axis_size("band")
    sub_count = lax.axis_size("sub")
    owners = plane_count * sub_count
    depth, grid = potential.shape[0], potential.shape[1]
    dev_slots, coef_slots = coefficients.shape[2], coefficients.shape[3]
    slots = stick_column.shape[0]
    devices = plane_count * band_count * sub_count
    wide = -(-(grid // 2 + 1) // LANES) * LANES
    span = -(-depth // 16) * 16
    block = max(k for k in range(1, 6) if depth % k == 0)
    sizes = (
        plane_count, band_count, sub_count, owners, depth, grid, slots, dev_slots, coef_slots, block
    )
    f32, bf16 = jnp.float32, jnp.bfloat16
    vmem = pl.BlockSpec(memory_space=pltpu.VMEM)
    return pl.pallas_call(
        functools.partial(fused_kernel, sizes),
        out_shape=jax.ShapeDtypeStruct(coefficients.shape, f32),
        in_specs=[pl.BlockSpec(memory_space=pltpu.HBM)] * 6,
        out_specs=vmem,
        scratch_shapes=[
            pltpu.SMEM(plane_start.shape, jnp.int32),
            pltpu.SMEM(stick_length.shape, jnp.int32),
            pltpu.VMEM((1, slots), jnp.int32),
            pltpu.VMEM((1, slots), jnp.int32),
            pltpu.VMEM(coefficients.shape, f32),
            pltpu.VMEM((owners * LANES, 2 * coef_slots), bf16),
            pltpu.VMEM((owners * LANES, 2 * coef_slots), bf16),
            pltpu.VMEM((devices, dev_slots, LANES), f32),
            pltpu.VMEM((devices, dev_slots, LANES), f32),
            pltpu.VMEM((devices, dev_slots, LANES), f32),
            pltpu.VMEM((devices, dev_slots, LANES), f32),
            pltpu.VMEM(potential.shape, f32),
            pltpu.VMEM((depth, grid, 2 * wide), f32),
            pltpu.VMEM((grid, slots), f32),
            pltpu.VMEM((grid, slots), f32),
            pltpu.VMEM((3 * slots, 2 * wide), bf16),
            pltpu.VMEM((2 * wide, 2 * slots), bf16),
            pltpu.VMEM((2, span, slots), f32),
            pltpu.VMEM((LANES, slots), f32),
            pltpu.SemaphoreType.DMA,
            pltpu.SemaphoreType.DMA((5,)),
            pltpu.SemaphoreType.DMA((2,)),
            pltpu.SemaphoreType.DMA((2,)),
        ],
        compiler_params=pltpu.CompilerParams(
            collective_id=0, has_side_effects=True, vmem_limit_bytes=64 * 1024 * 1024
        ),
        cost_estimate=pl.CostEstimate(
            flops=4 * depth * 2 * grid * slots * 2 * wide,
            bytes_accessed=potential.size * 4,
            transcendentals=0,
        ),
    )(
        plane_start,
        stick_length,
        stick_column.reshape(1, slots),
        stick_length.reshape(1, slots),
        coefficients,
        potential,
    )


two_pi = 2.0 * math.pi
precise = lax.Precision.HIGHEST


def phase_table(product, grid_size):
    angle = (product % grid_size).astype(jnp.float32) * (two_pi / grid_size)
    return (jnp.cos(angle), jnp.sin(angle))


def global_slot(owner_src, band_src, within, band_count, sub_count, dev_slots):
    return (
        (owner_src // sub_count * band_count + band_src) * sub_count + owner_src % sub_count
    ) * dev_slots + within


def inverse_columns(parts, lengths, line_cos, line_sin, plane_z, grid_size):
    live_mask = jnp.arange(parts.shape[3], dtype=jnp.int32)[None, :] < lengths[:, None]
    real_part = jnp.where(live_mask, parts[0], 0.0)
    imag_part = jnp.where(live_mask, parts[1], 0.0)
    first_real = jnp.einsum("bsl,lq->bqs", real_part, line_cos, precision=precise) - jnp.einsum(
        "bsl,lq->bqs", imag_part, line_sin, precision=precise
    )
    first_imag = jnp.einsum("bsl,lq->bqs", real_part, line_sin, precision=precise) + jnp.einsum(
        "bsl,lq->bqs", imag_part, line_cos, precision=precise
    )
    shift_cos, shift_sin = phase_table(plane_z[:, None] * (lengths // 2)[None, :], grid_size)
    out_real = first_real * shift_cos + first_imag * shift_sin
    out_imag = first_imag * shift_cos - first_real * shift_sin
    return jnp.stack([out_real, out_imag])


def forward_columns(data, lengths, line_cos, line_sin, plane_z, grid_size):
    shift_cos, shift_sin = phase_table(plane_z[:, None] * (lengths // 2)[None, :], grid_size)
    turn_real = data[0] * shift_cos - data[1] * shift_sin
    turn_imag = data[1] * shift_cos + data[0] * shift_sin
    out_real = jnp.einsum("bqs,lq->bsl", turn_real, line_cos, precision=precise) + jnp.einsum(
        "bqs,lq->bsl", turn_imag, line_sin, precision=precise
    )
    out_imag = jnp.einsum("bqs,lq->bsl", turn_imag, line_cos, precision=precise) - jnp.einsum(
        "bqs,lq->bsl", turn_real, line_sin, precision=precise
    )
    scale = 1.0 / float(grid_size * grid_size * grid_size)
    live_mask = jnp.arange(line_cos.shape[0], dtype=jnp.int32)[None, :] < lengths[:, None]
    return jnp.stack(
        [jnp.where(live_mask, out_real * scale, 0.0), jnp.where(live_mask, out_imag * scale, 0.0)]
    )


def complex_table(dft_cos, dft_sin, sign):
    from_real = jnp.stack([dft_cos, sign * dft_sin], axis=1)
    from_imag = jnp.stack([-sign * dft_sin, dft_cos], axis=1)
    return jnp.stack([from_real, from_imag])


def apply_planes(received, columns, potential, grid_size):
    depth_count = received.shape[1]
    radius = grid_size // 4
    compact = 2 * radius + 1
    col_x = columns // grid_size
    col_y = columns % grid_size
    small_x = jnp.where(col_x <= radius, col_x, col_x - grid_size + compact)
    small_y = jnp.where(col_y <= radius, col_y, col_y - grid_size + compact)
    small_index = small_x * compact + small_y
    spread = (
        jnp.zeros((2, depth_count, compact * compact), jnp.float32)
        .at[:, :, small_index]
        .add(received)
    )
    spread = jnp.transpose(spread.reshape(2, depth_count, compact, compact), (1, 2, 0, 3))
    small_axis = jnp.arange(compact, dtype=jnp.int32)
    wave_freq = jnp.where(small_axis <= radius, small_axis, small_axis - compact + grid_size)
    wave_index = jnp.arange(grid_size, dtype=jnp.int32)
    up_cos, up_sin = phase_table(wave_freq[:, None] * wave_index[None, :], grid_size)
    down_cos, down_sin = phase_table(wave_index[:, None] * wave_freq[None, :], grid_size)
    table_plus = complex_table(up_cos, up_sin, 1.0)
    table_minus = complex_table(down_cos, down_sin, -1.0)
    spread = jnp.einsum("zacb,cadx->zxdb", spread, table_plus, precision=precise)
    spread = jnp.einsum("zxcb,cbdk->zxdk", spread, table_plus, precision=precise)
    spread = spread * potential[:, :, None, :]
    spread = jnp.einsum("zxcy,cydk->zxdk", spread, table_minus, precision=precise)
    spread = jnp.einsum("zxcb,cxda->zadb", spread, table_minus, precision=precise)
    planes_flat = jnp.transpose(spread, (2, 0, 1, 3)).reshape(2, depth_count, compact * compact)
    return planes_flat[:, :, small_index]


def on_device(coefficients, potential, stick_column, stick_length, plane_start):
    plane_count = lax.axis_size("plane")
    band_count = lax.axis_size("band")
    sub_count = lax.axis_size("sub")
    owners_count = plane_count * sub_count
    plane_depth = potential.shape[0]
    grid_size = potential.shape[1]
    coef_slots = coefficients.shape[3]
    dev_slots = coefficients.shape[2]
    group_slots = band_count * dev_slots
    plane_pos = lax.axis_index("plane")
    sub_pos = lax.axis_index("sub")
    my_owner = plane_pos * sub_count + sub_pos
    plane_counts = plane_start[1:] - plane_start[:-1]
    depth_index = jnp.arange(plane_depth, dtype=jnp.int32)
    valid_plane = (depth_index[None, :] < plane_counts[:, None]).reshape(-1)
    plane_z = jnp.where(
        valid_plane, (plane_start[:-1][:, None] + depth_index[None, :]).reshape(-1), 0
    )
    line_index = jnp.arange(coef_slots, dtype=jnp.int32)
    line_cos, line_sin = phase_table(line_index[:, None] * plane_z[None, :], grid_size)
    valid_float = valid_plane.astype(jnp.float32)[None, :]
    line_cos = line_cos * valid_float
    line_sin = line_sin * valid_float
    owner_axis = jnp.arange(owners_count, dtype=jnp.int32)
    band_axis = jnp.arange(band_count, dtype=jnp.int32)
    within_axis = jnp.arange(dev_slots, dtype=jnp.int32)
    owner_major = global_slot(
        owner_axis[:, None, None],
        band_axis[None, :, None],
        within_axis[None, None, :],
        band_count,
        sub_count,
        dev_slots,
    ).reshape(-1)
    total_slots = owner_major.shape[0]
    question = plane_depth * owners_count
    group_ids = global_slot(
        my_owner, band_axis[:, None], within_axis[None, :], band_count, sub_count, dev_slots
    ).reshape(-1)
    group_len = stick_length[group_ids]
    regrouped = lax.all_to_all(coefficients, "band", split_axis=1, concat_axis=2, tiled=True)
    columns_z = inverse_columns(regrouped, group_len, line_cos, line_sin, plane_z, grid_size)
    columns_z = columns_z.reshape(2, 1, owners_count, plane_depth, group_slots)
    arrived = lax.all_to_all(columns_z, ("plane", "sub"), split_axis=2, concat_axis=4, tiled=True)
    planes_out = apply_planes(
        arrived.reshape(2, plane_depth, total_slots),
        stick_column[owner_major],
        potential,
        grid_size,
    )
    returned = lax.all_to_all(
        planes_out.reshape(2, 1, 1, plane_depth, total_slots),
        ("plane", "sub"),
        split_axis=4,
        concat_axis=2,
        tiled=True,
    )
    coef_back = forward_columns(
        returned.reshape(2, 1, question, group_slots),
        group_len,
        line_cos,
        line_sin,
        plane_z,
        grid_size,
    )
    applied = lax.all_to_all(coef_back, "band", split_axis=2, concat_axis=1, tiled=True)
    return applied


def on_device_any(coefficients, potential, stick_column, stick_length, plane_start):
    small = (
        stick_column.shape[0] <= 512 and potential.shape[0] <= HALF and coefficients.shape[2] == 8
    )
    chosen = on_device_fused if small else on_device
    return chosen(coefficients, potential, stick_column, stick_length, plane_start)


def solution(mesh):
    placed = (
        P(None, None, ("parts", "plane", "band", "sub"), None),
        P(("parts", "plane", "sub"), None, None),
        P(),
        P(),
        P(),
    )
    return jax.shard_map(
        on_device_any,
        mesh=mesh,
        in_specs=placed,
        out_specs=P(None, None, ("parts", "plane", "band", "sub"), None),
        check_vma=False,
    )
```

```python
import functools
import math

import jax
import jax.numpy as jnp
from jax import lax
from jax.experimental import pallas as pl
from jax.experimental.pallas import tpu as pltpu
from jax.sharding import PartitionSpec as P

LANES = 128
HALF = LANES // 2
SIN_TERMS = [(-1.0) ** k / math.factorial(2 * k + 1) for k in range(7)]
COS_TERMS = [(-1.0) ** k / math.factorial(2 * k) for k in range(8)]


def series(square, terms):
    total = jnp.full_like(square, terms[-1])
    for term in reversed(terms[:-1]):
        total = total * square + term
    return total


def phases(product, grid_size):
    turns = product * (1.0 / grid_size)
    rest = product - grid_size * jnp.floor(turns + 0.5)
    angle = rest * (math.pi / grid_size)
    square = angle * angle
    half_sin = angle * series(square, SIN_TERMS)
    half_cos = series(square, COS_TERMS)
    return 1.0 - 2.0 * half_sin * half_sin, 2.0 * half_sin * half_cos


def split(values):
    high = values.astype(jnp.bfloat16)
    low = (values - high.astype(jnp.float32)).astype(jnp.bfloat16)
    return high, low


def dot(left, right):
    return jnp.dot(left, right, preferred_element_type=jnp.float32)


def dot_rows(left, right):
    return lax.dot_general(
        left, right, (((1,), (1,)), ((), ())), preferred_element_type=jnp.float32
    )


def rows_of(shape):
    return lax.broadcasted_iota(jnp.int32, shape, 0)


def lanes_of(shape):
    return lax.broadcasted_iota(jnp.int32, shape, 1)


def whole(values, divisor):
    return jnp.floor((values + 0.5) * (1.0 / divisor))


def fused_kernel(
    sizes,
    start_hbm,
    length_hbm,
    column_row_hbm,
    length_row_hbm,
    coef_hbm,
    pot_hbm,
    out_ref,
    start_smem,
    length_smem,
    column_row,
    length_row,
    coef_ref,
    line_high,
    line_low,
    send_buf,
    recv_buf,
    ret_buf,
    back_buf,
    pot_vmem,
    combined,
    x_cos,
    x_sin,
    y_up,
    y_down,
    values,
    result,
    pot_sem,
    small_sem,
    out_sems,
    home_sems,
):
    plane_count, band_count, sub_count, owners, depth, grid, slots, dev_slots, coef_slots, block = sizes
    span = -(-depth // 16) * 16
    devices = plane_count * band_count * sub_count
    half_grid = grid // 2
    wide = y_down.shape[0] // 2

    part = lax.axis_index("parts")
    plane_pos = lax.axis_index("plane")
    band_pos = lax.axis_index("band")
    sub_pos = lax.axis_index("sub")
    me = (plane_pos * band_count + band_pos) * sub_count + sub_pos
    my_owner = plane_pos * sub_count + sub_pos

    def wrap(position, offset, count):
        moved = position + offset
        return jnp.where(moved >= count, moved - count, moved)

    def place(step):
        other_plane = wrap(plane_pos, step[0], plane_count)
        other_band = wrap(band_pos, step[1], band_count)
        other_sub = wrap(sub_pos, step[2], sub_count)
        owner = other_plane * sub_count + other_sub
        other = (other_plane * band_count + other_band) * sub_count + other_sub
        tile = owner * band_count + other_band
        return other, tile, (part, other_plane, other_band, other_sub)

    steps = [
        (p, b, s)
        for p in sorted(range(plane_count), key=lambda p: -min(p, plane_count - p))
        for b in reversed(range(band_count))
        for s in reversed(range(sub_count))
        if p + b + s > 0
    ]
    places = [place(step) for step in steps]
    my_tile = my_owner * band_count + band_pos

    small_copies = [
        pltpu.make_async_copy(source, target, small_sem.at[i])
        for i, (source, target) in enumerate(
            [
                (start_hbm, start_smem),
                (length_hbm, length_smem),
                (coef_hbm, coef_ref),
                (column_row_hbm, column_row),
                (length_row_hbm, length_row),
            ]
        )
    ]
    for copy in small_copies:
        copy.start()
    barrier = pltpu.get_barrier_semaphore()
    for _, _, device in places:
        pl.semaphore_signal(
            barrier, inc=1, device_id=device, device_id_type=pl.DeviceIdType.MESH
        )
    pot_copy = pltpu.make_async_copy(pot_hbm, pot_vmem, pot_sem)
    pot_copy.start()

    for copy in small_copies:
        copy.wait()

    def line_block(owner, carry):
        first = start_smem[owner]
        count = start_smem[owner + 1] - first
        shape = (span, coef_slots)
        row = rows_of(shape)
        product = (row + first).astype(jnp.float32) * lanes_of(shape).astype(jnp.float32)
        cos, sin = phases(product, float(grid))
        held = row < count
        cos = jnp.where(held, cos, 0.0)
        sin = jnp.where(held, sin, 0.0)
        blank = jnp.zeros((HALF - span, 2 * coef_slots), jnp.float32)
        rows = jnp.concatenate(
            [
                jnp.concatenate([cos, -sin], axis=1),
                blank,
                jnp.concatenate([sin, cos], axis=1),
                blank,
            ],
            axis=0,
        )
        high, low = split(rows)
        at = pl.ds(pl.multiple_of(owner * LANES, LANES), LANES)
        line_high[at, :] = high
        line_low[at, :] = low
        return carry

    lax.fori_loop(0, owners, line_block, 0, unroll=True)

    lane_small = lanes_of((dev_slots, coef_slots))
    row_small = rows_of((dev_slots, coef_slots))
    own_length = jnp.zeros((dev_slots, coef_slots), jnp.int32)
    for slot in range(dev_slots):
        own_length = jnp.where(row_small == slot, length_smem[me * dev_slots + slot], own_length)
    live = lane_small < own_length
    held = jnp.concatenate(
        [
            jnp.concatenate(
                [jnp.where(live, coef_ref[0, b], 0.0), jnp.where(live, coef_ref[1, b], 0.0)], axis=1
            )
            for b in range(band_count)
        ],
        axis=0,
    )
    high, low = split(held)
    both = dot_rows(jnp.concatenate([high, low], axis=0), line_high[...])
    rows = band_count * dev_slots
    sent = both[:rows] + both[rows:] + dot_rows(high, line_low[...])
    for owner in range(owners):
        for b in range(band_count):
            send_buf[owner * band_count + b] = sent[
                b * dev_slots : (b + 1) * dev_slots, owner * LANES : (owner + 1) * LANES
            ]

    pl.semaphore_wait(barrier, devices - 1)

    def send(source, target, sems, device):
        return pltpu.make_async_remote_copy(
            src_ref=source,
            dst_ref=target,
            send_sem=sems.at[0],
            recv_sem=sems.at[1],
            device_id=device,
            device_id_type=pl.DeviceIdType.MESH,
        )

    def all_of(buffer, sems):
        others = buffer.at[pl.ds(0, devices - 1)]
        return send(others, others, sems, places[0][2])

    for _, tile, device in places:
        send(send_buf.at[tile], recv_buf.at[me], out_sems, device).start()
    recv_buf[me] = send_buf[my_tile]

    column = column_row[...].astype(jnp.float32)
    column_x = whole(column, grid)
    column_y = column - grid * column_x
    cos, sin = phases(rows_of((grid, slots)).astype(jnp.float32) * column_x, float(grid))
    x_cos[...] = cos
    x_sin[...] = sin
    cos, sin = phases(rows_of((wide, slots)).astype(jnp.float32) * column_y, float(grid))
    high, low = split(jnp.concatenate([cos, sin], axis=0))
    y_down[:, :slots] = high
    y_down[:, slots:] = low
    high, low = split(jnp.concatenate([cos.T, sin.T], axis=1))
    y_up[:slots] = high
    y_up[slots : 2 * slots] = high
    y_up[2 * slots :] = low
    half_length = whole(length_row[...].astype(jnp.float32), 2)
    my_first = start_smem[my_owner]
    turn_cos, turn_sin = phases(
        (rows_of((span, slots)) + my_first).astype(jnp.float32) * half_length, float(grid)
    )

    row = rows_of((grid, wide))
    lane = lanes_of((grid, wide))
    same = jnp.where((row == lane) & (lane <= half_grid), 1.0, 0.0)
    mirror = jnp.where((row + lane == grid) & (lane < half_grid), 1.0, 0.0)
    inner = jnp.where((row == lane) & (lane < half_grid) & (lane > 0), 1.0, 0.0)
    pairing = jnp.concatenate([same + mirror, inner - mirror], axis=1).astype(jnp.bfloat16)
    pot_copy.wait()

    def combine(step, carry):
        for i in range(block):
            z = step * block + i
            high, low = split(pot_vmem[z])
            combined[z] = dot(high, pairing) + dot(low, pairing)
        return carry

    lax.fori_loop(0, depth // block, combine, 0)
    result[...] = jnp.zeros_like(result)

    all_of(recv_buf, out_sems).wait_recv()
    turned = recv_buf[...].reshape(slots, LANES).T
    got_real = turned[:span]
    got_imag = turned[HALF : HALF + span]
    values[0] = got_real * turn_cos + got_imag * turn_sin
    values[1] = got_imag * turn_cos - got_real * turn_sin

    def planes(step, carry):
        for i in range(depth):
            z = i
            real = values[0, pl.ds(z, 1), :]
            imag = values[1, pl.ds(z, 1), :]
            ax = x_cos[...]
            bx = x_sin[...]
            high, low = split(
                jnp.concatenate([ax * real - bx * imag, ax * imag + bx * real], axis=0)
            )
            psi = dot(jnp.concatenate([high, low, high], axis=1), y_up[...])
            even_real, odd_real = psi[:grid, :wide], psi[:grid, wide:]
            even_imag, odd_imag = psi[grid:, :wide], psi[grid:, wide:]
            even = combined[z, :, :wide]
            odd = combined[z, :, wide:]
            product = jnp.concatenate(
                [
                    jnp.concatenate(
                        [
                            even * even_real - odd * odd_imag,
                            odd * even_imag + even * odd_real,
                        ],
                        axis=1,
                    ),
                    jnp.concatenate(
                        [
                            even * even_imag + odd * odd_real,
                            even * odd_imag - odd * even_real,
                        ],
                        axis=1,
                    ),
                ],
                axis=0,
            )
            high, low = split(product)
            first = dot(high, y_down[...])
            back = first[:, :slots] + first[:, slots:] + dot(low, y_down[:, :slots])
            back_real, back_imag = back[:grid], back[grid:]
            result[pl.ds(z, 1), :] = jnp.sum(ax * back_real + bx * back_imag, axis=0, keepdims=True)
            result[pl.ds(HALF + z, 1), :] = jnp.sum(
                ax * back_imag - bx * back_real, axis=0, keepdims=True
            )
        return carry

    planes(0, 0)

    out_real = result[:span]
    out_imag = result[HALF : HALF + span]
    blank = jnp.zeros((HALF - span, slots), jnp.float32)
    ret_buf[...] = jnp.concatenate(
        [
            out_real * turn_cos - out_imag * turn_sin,
            blank,
            out_imag * turn_cos + out_real * turn_sin,
            blank,
        ],
        axis=0,
    ).T.reshape(devices, dev_slots, LANES)
    for other, _, device in places:
        send(ret_buf.at[other], back_buf.at[my_tile], home_sems, device).start()
    back_buf[my_tile] = ret_buf[me]
    all_of(back_buf, home_sems).wait_recv()

    lines = jnp.concatenate(
        [
            jnp.concatenate([back_buf[owner * band_count + b] for b in range(band_count)], axis=0)
            for owner in range(owners)
        ],
        axis=1,
    )
    high, low = split(lines)
    both = dot(jnp.concatenate([high, low], axis=0), line_high[...])
    applied = both[:rows] + both[rows:] + dot(high, line_low[...])
    applied = applied * (1.0 / float(grid * grid * grid))
    for b in range(band_count):
        for c in range(2):
            piece = applied[
                b * dev_slots : (b + 1) * dev_slots, c * coef_slots : (c + 1) * coef_slots
            ]
            out_ref[c, b] = jnp.where(live, piece, 0.0)

    all_of(send_buf, out_sems).wait_send()
    all_of(ret_buf, home_sems).wait_send()


def on_device_fused(coefficients, potential, stick_column, stick_length, plane_start):
    plane_count = lax.axis_size("plane")
    band_count = lax.axis_size("band")
    sub_count = lax.axis_size("sub")
    owners = plane_count * sub_count
    depth, grid = potential.shape[0], potential.shape[1]
    dev_slots, coef_slots = coefficients.shape[2], coefficients.shape[3]
    slots = stick_column.shape[0]
    devices = plane_count * band_count * sub_count
    wide = -(-(grid // 2 + 1) // LANES) * LANES
    span = -(-depth // 16) * 16
    block = max(k for k in range(1, 6) if depth % k == 0)
    sizes = (
        plane_count, band_count, sub_count, owners, depth, grid, slots, dev_slots, coef_slots, block
    )
    f32, bf16 = jnp.float32, jnp.bfloat16
    vmem = pl.BlockSpec(memory_space=pltpu.VMEM)
    return pl.pallas_call(
        functools.partial(fused_kernel, sizes),
        out_shape=jax.ShapeDtypeStruct(coefficients.shape, f32),
        in_specs=[pl.BlockSpec(memory_space=pltpu.HBM)] * 6,
        out_specs=vmem,
        scratch_shapes=[
            pltpu.SMEM(plane_start.shape, jnp.int32),
            pltpu.SMEM(stick_length.shape, jnp.int32),
            pltpu.VMEM((1, slots), jnp.int32),
            pltpu.VMEM((1, slots), jnp.int32),
            pltpu.VMEM(coefficients.shape, f32),
            pltpu.VMEM((owners * LANES, 2 * coef_slots), bf16),
            pltpu.VMEM((owners * LANES, 2 * coef_slots), bf16),
            pltpu.VMEM((devices, dev_slots, LANES), f32),
            pltpu.VMEM((devices, dev_slots, LANES), f32),
            pltpu.VMEM((devices, dev_slots, LANES), f32),
            pltpu.VMEM((devices, dev_slots, LANES), f32),
            pltpu.VMEM(potential.shape, f32),
            pltpu.VMEM((depth, grid, 2 * wide), f32),
            pltpu.VMEM((grid, slots), f32),
            pltpu.VMEM((grid, slots), f32),
            pltpu.VMEM((3 * slots, 2 * wide), bf16),
            pltpu.VMEM((2 * wide, 2 * slots), bf16),
            pltpu.VMEM((2, span, slots), f32),
            pltpu.VMEM((LANES, slots), f32),
            pltpu.SemaphoreType.DMA,
            pltpu.SemaphoreType.DMA((5,)),
            pltpu.SemaphoreType.DMA((2,)),
            pltpu.SemaphoreType.DMA((2,)),
        ],
        compiler_params=pltpu.CompilerParams(
            collective_id=0, has_side_effects=True, vmem_limit_bytes=64 * 1024 * 1024
        ),
        cost_estimate=pl.CostEstimate(
            flops=4 * depth * 2 * grid * slots * 2 * wide,
            bytes_accessed=potential.size * 4,
            transcendentals=0,
        ),
    )(
        plane_start,
        stick_length,
        stick_column.reshape(1, slots),
        stick_length.reshape(1, slots),
        coefficients,
        potential,
    )


two_pi = 2.0 * math.pi
precise = lax.Precision.HIGHEST


def phase_table(product, grid_size):
    angle = (product % grid_size).astype(jnp.float32) * (two_pi / grid_size)
    return (jnp.cos(angle), jnp.sin(angle))


def global_slot(owner_src, band_src, within, band_count, sub_count, dev_slots):
    return (
        (owner_src // sub_count * band_count + band_src) * sub_count + owner_src % sub_count
    ) * dev_slots + within


def inverse_columns(parts, lengths, line_cos, line_sin, plane_z, grid_size):
    live_mask = jnp.arange(parts.shape[3], dtype=jnp.int32)[None, :] < lengths[:, None]
    real_part = jnp.where(live_mask, parts[0], 0.0)
    imag_part = jnp.where(live_mask, parts[1], 0.0)
    first_real = jnp.einsum("bsl,lq->bqs", real_part, line_cos, precision=precise) - jnp.einsum(
        "bsl,lq->bqs", imag_part, line_sin, precision=precise
    )
    first_imag = jnp.einsum("bsl,lq->bqs", real_part, line_sin, precision=precise) + jnp.einsum(
        "bsl,lq->bqs", imag_part, line_cos, precision=precise
    )
    shift_cos, shift_sin = phase_table(plane_z[:, None] * (lengths // 2)[None, :], grid_size)
    out_real = first_real * shift_cos + first_imag * shift_sin
    out_imag = first_imag * shift_cos - first_real * shift_sin
    return jnp.stack([out_real, out_imag])


def forward_columns(data, lengths, line_cos, line_sin, plane_z, grid_size):
    shift_cos, shift_sin = phase_table(plane_z[:, None] * (lengths // 2)[None, :], grid_size)
    turn_real = data[0] * shift_cos - data[1] * shift_sin
    turn_imag = data[1] * shift_cos + data[0] * shift_sin
    out_real = jnp.einsum("bqs,lq->bsl", turn_real, line_cos, precision=precise) + jnp.einsum(
        "bqs,lq->bsl", turn_imag, line_sin, precision=precise
    )
    out_imag = jnp.einsum("bqs,lq->bsl", turn_imag, line_cos, precision=precise) - jnp.einsum(
        "bqs,lq->bsl", turn_real, line_sin, precision=precise
    )
    scale = 1.0 / float(grid_size * grid_size * grid_size)
    live_mask = jnp.arange(line_cos.shape[0], dtype=jnp.int32)[None, :] < lengths[:, None]
    return jnp.stack(
        [jnp.where(live_mask, out_real * scale, 0.0), jnp.where(live_mask, out_imag * scale, 0.0)]
    )


def complex_table(dft_cos, dft_sin, sign):
    from_real = jnp.stack([dft_cos, sign * dft_sin], axis=1)
    from_imag = jnp.stack([-sign * dft_sin, dft_cos], axis=1)
    return jnp.stack([from_real, from_imag])


def apply_planes(received, columns, potential, grid_size):
    depth_count = received.shape[1]
    radius = grid_size // 4
    compact = 2 * radius + 1
    col_x = columns // grid_size
    col_y = columns % grid_size
    small_x = jnp.where(col_x <= radius, col_x, col_x - grid_size + compact)
    small_y = jnp.where(col_y <= radius, col_y, col_y - grid_size + compact)
    small_index = small_x * compact + small_y
    spread = (
        jnp.zeros((2, depth_count, compact * compact), jnp.float32)
        .at[:, :, small_index]
        .add(received)
    )
    spread = jnp.transpose(spread.reshape(2, depth_count, compact, compact), (1, 2, 0, 3))
    small_axis = jnp.arange(compact, dtype=jnp.int32)
    wave_freq = jnp.where(small_axis <= radius, small_axis, small_axis - compact + grid_size)
    wave_index = jnp.arange(grid_size, dtype=jnp.int32)
    up_cos, up_sin = phase_table(wave_freq[:, None] * wave_index[None, :], grid_size)
    down_cos, down_sin = phase_table(wave_index[:, None] * wave_freq[None, :], grid_size)
    table_plus = complex_table(up_cos, up_sin, 1.0)
    table_minus = complex_table(down_cos, down_sin, -1.0)
    spread = jnp.einsum("zacb,cadx->zxdb", spread, table_plus, precision=precise)
    spread = jnp.einsum("zxcb,cbdk->zxdk", spread, table_plus, precision=precise)
    spread = spread * potential[:, :, None, :]
    spread = jnp.einsum("zxcy,cydk->zxdk", spread, table_minus, precision=precise)
    spread = jnp.einsum("zxcb,cxda->zadb", spread, table_minus, precision=precise)
    planes_flat = jnp.transpose(spread, (2, 0, 1, 3)).reshape(2, depth_count, compact * compact)
    return planes_flat[:, :, small_index]


def on_device(coefficients, potential, stick_column, stick_length, plane_start):
    plane_count = lax.axis_size("plane")
    band_count = lax.axis_size("band")
    sub_count = lax.axis_size("sub")
    owners_count = plane_count * sub_count
    plane_depth = potential.shape[0]
    grid_size = potential.shape[1]
    coef_slots = coefficients.shape[3]
    dev_slots = coefficients.shape[2]
    group_slots = band_count * dev_slots
    plane_pos = lax.axis_index("plane")
    sub_pos = lax.axis_index("sub")
    my_owner = plane_pos * sub_count + sub_pos
    plane_counts = plane_start[1:] - plane_start[:-1]
    depth_index = jnp.arange(plane_depth, dtype=jnp.int32)
    valid_plane = (depth_index[None, :] < plane_counts[:, None]).reshape(-1)
    plane_z = jnp.where(
        valid_plane, (plane_start[:-1][:, None] + depth_index[None, :]).reshape(-1), 0
    )
    line_index = jnp.arange(coef_slots, dtype=jnp.int32)
    line_cos, line_sin = phase_table(line_index[:, None] * plane_z[None, :], grid_size)
    valid_float = valid_plane.astype(jnp.float32)[None, :]
    line_cos = line_cos * valid_float
    line_sin = line_sin * valid_float
    owner_axis = jnp.arange(owners_count, dtype=jnp.int32)
    band_axis = jnp.arange(band_count, dtype=jnp.int32)
    within_axis = jnp.arange(dev_slots, dtype=jnp.int32)
    owner_major = global_slot(
        owner_axis[:, None, None],
        band_axis[None, :, None],
        within_axis[None, None, :],
        band_count,
        sub_count,
        dev_slots,
    ).reshape(-1)
    total_slots = owner_major.shape[0]
    question = plane_depth * owners_count
    group_ids = global_slot(
        my_owner, band_axis[:, None], within_axis[None, :], band_count, sub_count, dev_slots
    ).reshape(-1)
    group_len = stick_length[group_ids]
    regrouped = lax.all_to_all(coefficients, "band", split_axis=1, concat_axis=2, tiled=True)
    columns_z = inverse_columns(regrouped, group_len, line_cos, line_sin, plane_z, grid_size)
    columns_z = columns_z.reshape(2, 1, owners_count, plane_depth, group_slots)
    arrived = lax.all_to_all(columns_z, ("plane", "sub"), split_axis=2, concat_axis=4, tiled=True)
    planes_out = apply_planes(
        arrived.reshape(2, plane_depth, total_slots),
        stick_column[owner_major],
        potential,
        grid_size,
    )
    returned = lax.all_to_all(
        planes_out.reshape(2, 1, 1, plane_depth, total_slots),
        ("plane", "sub"),
        split_axis=4,
        concat_axis=2,
        tiled=True,
    )
    coef_back = forward_columns(
        returned.reshape(2, 1, question, group_slots),
        group_len,
        line_cos,
        line_sin,
        plane_z,
        grid_size,
    )
    applied = lax.all_to_all(coef_back, "band", split_axis=2, concat_axis=1, tiled=True)
    return applied


def on_device_any(coefficients, potential, stick_column, stick_length, plane_start):
    small = (
        stick_column.shape[0] <= 512 and potential.shape[0] <= HALF and coefficients.shape[2] == 8
    )
    chosen = on_device_fused if small else on_device
    return chosen(coefficients, potential, stick_column, stick_length, plane_start)


def solution(mesh):
    placed = (
        P(None, None, ("parts", "plane", "band", "sub"), None),
        P(("parts", "plane", "sub"), None, None),
        P(),
        P(),
        P(),
    )
    return jax.shard_map(
        on_device_any,
        mesh=mesh,
        in_specs=placed,
        out_specs=P(None, None, ("parts", "plane", "band", "sub"), None),
        check_vma=False,
    )
```

```python
import functools
import math

import jax
import jax.numpy as jnp
from jax import lax
from jax.experimental import pallas as pl
from jax.experimental.pallas import tpu as pltpu
from jax.sharding import PartitionSpec as P

LANES = 128
HALF = LANES // 2
SIN_TERMS = [(-1.0) ** k / math.factorial(2 * k + 1) for k in range(7)]
COS_TERMS = [(-1.0) ** k / math.factorial(2 * k) for k in range(8)]


def series(square, terms):
    total = jnp.full_like(square, terms[-1])
    for term in reversed(terms[:-1]):
        total = total * square + term
    return total


def phases(product, grid_size):
    turns = product * (1.0 / grid_size)
    rest = product - grid_size * jnp.floor(turns + 0.5)
    angle = rest * (math.pi / grid_size)
    square = angle * angle
    half_sin = angle * series(square, SIN_TERMS)
    half_cos = series(square, COS_TERMS)
    return 1.0 - 2.0 * half_sin * half_sin, 2.0 * half_sin * half_cos


def split(values):
    high = values.astype(jnp.bfloat16)
    low = (values - high.astype(jnp.float32)).astype(jnp.bfloat16)
    return high, low


def dot(left, right):
    return jnp.dot(left, right, preferred_element_type=jnp.float32)


def dot_rows(left, right):
    return lax.dot_general(
        left, right, (((1,), (1,)), ((), ())), preferred_element_type=jnp.float32
    )


def rows_of(shape):
    return lax.broadcasted_iota(jnp.int32, shape, 0)


def lanes_of(shape):
    return lax.broadcasted_iota(jnp.int32, shape, 1)


def whole(values, divisor):
    return jnp.floor((values + 0.5) * (1.0 / divisor))


def fused_kernel(
    sizes,
    start_hbm,
    length_hbm,
    column_row_hbm,
    length_row_hbm,
    coef_hbm,
    pot_hbm,
    out_ref,
    start_smem,
    length_smem,
    column_row,
    length_row,
    coef_ref,
    line_high,
    line_low,
    send_buf,
    recv_buf,
    ret_buf,
    back_buf,
    pot_vmem,
    combined,
    x_cos,
    x_sin,
    y_up,
    y_down,
    values,
    result,
    pot_sem,
    small_sem,
    out_sems,
    home_sems,
):
    plane_count, band_count, sub_count, owners, depth, grid, slots, dev_slots, coef_slots, block = sizes
    span = -(-depth // 16) * 16
    devices = plane_count * band_count * sub_count
    half_grid = grid // 2
    wide = y_down.shape[0] // 2

    part = lax.axis_index("parts")
    plane_pos = lax.axis_index("plane")
    band_pos = lax.axis_index("band")
    sub_pos = lax.axis_index("sub")
    me = (plane_pos * band_count + band_pos) * sub_count + sub_pos
    my_owner = plane_pos * sub_count + sub_pos

    def wrap(position, offset, count):
        moved = position + offset
        return jnp.where(moved >= count, moved - count, moved)

    def place(step):
        other_plane = wrap(plane_pos, step[0], plane_count)
        other_band = wrap(band_pos, step[1], band_count)
        other_sub = wrap(sub_pos, step[2], sub_count)
        owner = other_plane * sub_count + other_sub
        other = (other_plane * band_count + other_band) * sub_count + other_sub
        tile = owner * band_count + other_band
        return other, tile, (part, other_plane, other_band, other_sub)

    steps = [
        (p, b, s)
        for p in sorted(range(plane_count), key=lambda p: -min(p, plane_count - p))
        for b in reversed(range(band_count))
        for s in reversed(range(sub_count))
        if p + b + s > 0
    ]
    places = [place(step) for step in steps]
    my_tile = my_owner * band_count + band_pos

    small_copies = [
        pltpu.make_async_copy(source, target, small_sem.at[i])
        for i, (source, target) in enumerate(
            [
                (start_hbm, start_smem),
                (length_hbm, length_smem),
                (coef_hbm, coef_ref),
                (column_row_hbm, column_row),
                (length_row_hbm, length_row),
            ]
        )
    ]
    for copy in small_copies:
        copy.start()
    barrier = pltpu.get_barrier_semaphore()
    for _, _, device in places:
        pl.semaphore_signal(
            barrier, inc=1, device_id=device, device_id_type=pl.DeviceIdType.MESH
        )
    pot_copy = pltpu.make_async_copy(pot_hbm, pot_vmem, pot_sem)
    pot_copy.start()

    for copy in small_copies:
        copy.wait()

    def line_block(owner, carry):
        first = start_smem[owner]
        count = start_smem[owner + 1] - first
        shape = (span, coef_slots)
        row = rows_of(shape)
        product = (row + first).astype(jnp.float32) * lanes_of(shape).astype(jnp.float32)
        cos, sin = phases(product, float(grid))
        held = row < count
        cos = jnp.where(held, cos, 0.0)
        sin = jnp.where(held, sin, 0.0)
        blank = jnp.zeros((HALF - span, 2 * coef_slots), jnp.float32)
        rows = jnp.concatenate(
            [
                jnp.concatenate([cos, -sin], axis=1),
                blank,
                jnp.concatenate([sin, cos], axis=1),
                blank,
            ],
            axis=0,
        )
        high, low = split(rows)
        at = pl.ds(pl.multiple_of(owner * LANES, LANES), LANES)
        line_high[at, :] = high
        line_low[at, :] = low
        return carry

    lax.fori_loop(0, owners, line_block, 0, unroll=True)

    lane_small = lanes_of((dev_slots, coef_slots))
    row_small = rows_of((dev_slots, coef_slots))
    own_length = jnp.zeros((dev_slots, coef_slots), jnp.int32)
    for slot in range(dev_slots):
        own_length = jnp.where(row_small == slot, length_smem[me * dev_slots + slot], own_length)
    live = lane_small < own_length
    held = jnp.concatenate(
        [
            jnp.concatenate(
                [jnp.where(live, coef_ref[0, b], 0.0), jnp.where(live, coef_ref[1, b], 0.0)], axis=1
            )
            for b in range(band_count)
        ],
        axis=0,
    )
    high, low = split(held)
    both = dot_rows(jnp.concatenate([high, low], axis=0), line_high[...])
    rows = band_count * dev_slots
    sent = both[:rows] + both[rows:] + dot_rows(high, line_low[...])
    for owner in range(owners):
        for b in range(band_count):
            send_buf[owner * band_count + b] = sent[
                b * dev_slots : (b + 1) * dev_slots, owner * LANES : (owner + 1) * LANES
            ]

    pl.semaphore_wait(barrier, devices - 1)

    def send(source, target, sems, device):
        return pltpu.make_async_remote_copy(
            src_ref=source,
            dst_ref=target,
            send_sem=sems.at[0],
            recv_sem=sems.at[1],
            device_id=device,
            device_id_type=pl.DeviceIdType.MESH,
        )

    def all_of(buffer, sems):
        others = buffer.at[pl.ds(0, devices - 1)]
        return send(others, others, sems, places[0][2])

    for _, tile, device in places:
        send(send_buf.at[tile], recv_buf.at[me], out_sems, device).start()
    recv_buf[me] = send_buf[my_tile]

    column = column_row[...].astype(jnp.float32)
    column_x = whole(column, grid)
    column_y = column - grid * column_x
    cos, sin = phases(rows_of((grid, slots)).astype(jnp.float32) * column_x, float(grid))
    x_cos[...] = cos
    x_sin[...] = sin
    cos, sin = phases(rows_of((wide, slots)).astype(jnp.float32) * column_y, float(grid))
    high, low = split(jnp.concatenate([cos, sin], axis=0))
    y_down[:, :slots] = high
    y_down[:, slots:] = low
    high, low = split(jnp.concatenate([cos.T, sin.T], axis=1))
    y_up[:slots] = high
    y_up[slots : 2 * slots] = high
    y_up[2 * slots :] = low
    half_length = whole(length_row[...].astype(jnp.float32), 2)
    my_first = start_smem[my_owner]
    turn_cos, turn_sin = phases(
        (rows_of((span, slots)) + my_first).astype(jnp.float32) * half_length, float(grid)
    )

    row = rows_of((grid, wide))
    lane = lanes_of((grid, wide))
    same = jnp.where((row == lane) & (lane <= half_grid), 1.0, 0.0)
    mirror = jnp.where((row + lane == grid) & (lane < half_grid), 1.0, 0.0)
    inner = jnp.where((row == lane) & (lane < half_grid) & (lane > 0), 1.0, 0.0)
    pairing = jnp.concatenate([same + mirror, inner - mirror], axis=1).astype(jnp.bfloat16)
    pot_copy.wait()

    def combine(step, carry):
        for i in range(block):
            z = step * block + i
            high, low = split(pot_vmem[z])
            combined[z] = dot(high, pairing) + dot(low, pairing)
        return carry

    lax.fori_loop(0, depth // block, combine, 0)
    result[...] = jnp.zeros_like(result)

    all_of(recv_buf, out_sems).wait_recv()
    turned = recv_buf[...].reshape(slots, LANES).T
    got_real = turned[:span]
    got_imag = turned[HALF : HALF + span]
    values[0] = got_real * turn_cos + got_imag * turn_sin
    values[1] = got_imag * turn_cos - got_real * turn_sin

    def planes(first):
        ax = x_cos[...]
        bx = x_sin[...]
        group = range(first, first + block)
        parts = []
        for z in group:
            real = values[0, pl.ds(z, 1), :]
            imag = values[1, pl.ds(z, 1), :]
            parts += [ax * real - bx * imag, ax * imag + bx * real]
        high, low = split(jnp.concatenate(parts, axis=0))
        both_psi = dot(jnp.concatenate([high, low, high], axis=1), y_up[...])
        parts = []
        for i, z in enumerate(group):
            psi = both_psi[2 * i * grid : 2 * (i + 1) * grid]
            even_real, odd_real = psi[:grid, :wide], psi[:grid, wide:]
            even_imag, odd_imag = psi[grid:, :wide], psi[grid:, wide:]
            even = combined[z, :, :wide]
            odd = combined[z, :, wide:]
            product_real = [
                even * even_real - odd * odd_imag,
                odd * even_imag + even * odd_real,
            ]
            product_imag = [
                even * even_imag + odd * odd_real,
                even * odd_imag - odd * even_real,
            ]
            parts += [
                jnp.concatenate(product_real, axis=1),
                jnp.concatenate(product_imag, axis=1),
            ]
        high, low = split(jnp.concatenate(parts, axis=0))
        once = dot(high, y_down[...])
        back = once[:, :slots] + once[:, slots:] + dot(low, y_down[:, :slots])
        for i, z in enumerate(group):
            back_real = back[2 * i * grid : (2 * i + 1) * grid]
            back_imag = back[(2 * i + 1) * grid : 2 * (i + 1) * grid]
            result[pl.ds(z, 1), :] = jnp.sum(ax * back_real + bx * back_imag, axis=0, keepdims=True)
            result[pl.ds(HALF + z, 1), :] = jnp.sum(
                ax * back_imag - bx * back_real, axis=0, keepdims=True
            )

    for first in range(0, depth, block):
        planes(first)

    out_real = result[:span]
    out_imag = result[HALF : HALF + span]
    blank = jnp.zeros((HALF - span, slots), jnp.float32)
    ret_buf[...] = jnp.concatenate(
        [
            out_real * turn_cos - out_imag * turn_sin,
            blank,
            out_imag * turn_cos + out_real * turn_sin,
            blank,
        ],
        axis=0,
    ).T.reshape(devices, dev_slots, LANES)
    for other, _, device in places:
        send(ret_buf.at[other], back_buf.at[my_tile], home_sems, device).start()
    back_buf[my_tile] = ret_buf[me]
    all_of(back_buf, home_sems).wait_recv()

    lines = jnp.concatenate(
        [
            jnp.concatenate([back_buf[owner * band_count + b] for b in range(band_count)], axis=0)
            for owner in range(owners)
        ],
        axis=1,
    )
    high, low = split(lines)
    both = dot(jnp.concatenate([high, low], axis=0), line_high[...])
    applied = both[:rows] + both[rows:] + dot(high, line_low[...])
    applied = applied * (1.0 / float(grid * grid * grid))
    for b in range(band_count):
        for c in range(2):
            piece = applied[
                b * dev_slots : (b + 1) * dev_slots, c * coef_slots : (c + 1) * coef_slots
            ]
            out_ref[c, b] = jnp.where(live, piece, 0.0)

    all_of(send_buf, out_sems).wait_send()
    all_of(ret_buf, home_sems).wait_send()


def on_device_fused(coefficients, potential, stick_column, stick_length, plane_start):
    plane_count = lax.axis_size("plane")
    band_count = lax.axis_size("band")
    sub_count = lax.axis_size("sub")
    owners = plane_count * sub_count
    depth, grid = potential.shape[0], potential.shape[1]
    dev_slots, coef_slots = coefficients.shape[2], coefficients.shape[3]
    slots = stick_column.shape[0]
    devices = plane_count * band_count * sub_count
    wide = -(-(grid // 2 + 1) // LANES) * LANES
    span = -(-depth // 16) * 16
    block = max(k for k in range(1, 6) if depth % k == 0)
    sizes = (
        plane_count, band_count, sub_count, owners, depth, grid, slots, dev_slots, coef_slots, block
    )
    f32, bf16 = jnp.float32, jnp.bfloat16
    vmem = pl.BlockSpec(memory_space=pltpu.VMEM)
    return pl.pallas_call(
        functools.partial(fused_kernel, sizes),
        out_shape=jax.ShapeDtypeStruct(coefficients.shape, f32),
        in_specs=[pl.BlockSpec(memory_space=pltpu.HBM)] * 6,
        out_specs=vmem,
        scratch_shapes=[
            pltpu.SMEM(plane_start.shape, jnp.int32),
            pltpu.SMEM(stick_length.shape, jnp.int32),
            pltpu.VMEM((1, slots), jnp.int32),
            pltpu.VMEM((1, slots), jnp.int32),
            pltpu.VMEM(coefficients.shape, f32),
            pltpu.VMEM((owners * LANES, 2 * coef_slots), bf16),
            pltpu.VMEM((owners * LANES, 2 * coef_slots), bf16),
            pltpu.VMEM((devices, dev_slots, LANES), f32),
            pltpu.VMEM((devices, dev_slots, LANES), f32),
            pltpu.VMEM((devices, dev_slots, LANES), f32),
            pltpu.VMEM((devices, dev_slots, LANES), f32),
            pltpu.VMEM(potential.shape, f32),
            pltpu.VMEM((depth, grid, 2 * wide), f32),
            pltpu.VMEM((grid, slots), f32),
            pltpu.VMEM((grid, slots), f32),
            pltpu.VMEM((3 * slots, 2 * wide), bf16),
            pltpu.VMEM((2 * wide, 2 * slots), bf16),
            pltpu.VMEM((2, span, slots), f32),
            pltpu.VMEM((LANES, slots), f32),
            pltpu.SemaphoreType.DMA,
            pltpu.SemaphoreType.DMA((5,)),
            pltpu.SemaphoreType.DMA((2,)),
            pltpu.SemaphoreType.DMA((2,)),
        ],
        compiler_params=pltpu.CompilerParams(
            collective_id=0, has_side_effects=True, vmem_limit_bytes=64 * 1024 * 1024
        ),
        cost_estimate=pl.CostEstimate(
            flops=4 * depth * 2 * grid * slots * 2 * wide,
            bytes_accessed=potential.size * 4,
            transcendentals=0,
        ),
    )(
        plane_start,
        stick_length,
        stick_column.reshape(1, slots),
        stick_length.reshape(1, slots),
        coefficients,
        potential,
    )


two_pi = 2.0 * math.pi
precise = lax.Precision.HIGHEST


def phase_table(product, grid_size):
    angle = (product % grid_size).astype(jnp.float32) * (two_pi / grid_size)
    return (jnp.cos(angle), jnp.sin(angle))


def global_slot(owner_src, band_src, within, band_count, sub_count, dev_slots):
    return (
        (owner_src // sub_count * band_count + band_src) * sub_count + owner_src % sub_count
    ) * dev_slots + within


def inverse_columns(parts, lengths, line_cos, line_sin, plane_z, grid_size):
    live_mask = jnp.arange(parts.shape[3], dtype=jnp.int32)[None, :] < lengths[:, None]
    real_part = jnp.where(live_mask, parts[0], 0.0)
    imag_part = jnp.where(live_mask, parts[1], 0.0)
    first_real = jnp.einsum("bsl,lq->bqs", real_part, line_cos, precision=precise) - jnp.einsum(
        "bsl,lq->bqs", imag_part, line_sin, precision=precise
    )
    first_imag = jnp.einsum("bsl,lq->bqs", real_part, line_sin, precision=precise) + jnp.einsum(
        "bsl,lq->bqs", imag_part, line_cos, precision=precise
    )
    shift_cos, shift_sin = phase_table(plane_z[:, None] * (lengths // 2)[None, :], grid_size)
    out_real = first_real * shift_cos + first_imag * shift_sin
    out_imag = first_imag * shift_cos - first_real * shift_sin
    return jnp.stack([out_real, out_imag])


def forward_columns(data, lengths, line_cos, line_sin, plane_z, grid_size):
    shift_cos, shift_sin = phase_table(plane_z[:, None] * (lengths // 2)[None, :], grid_size)
    turn_real = data[0] * shift_cos - data[1] * shift_sin
    turn_imag = data[1] * shift_cos + data[0] * shift_sin
    out_real = jnp.einsum("bqs,lq->bsl", turn_real, line_cos, precision=precise) + jnp.einsum(
        "bqs,lq->bsl", turn_imag, line_sin, precision=precise
    )
    out_imag = jnp.einsum("bqs,lq->bsl", turn_imag, line_cos, precision=precise) - jnp.einsum(
        "bqs,lq->bsl", turn_real, line_sin, precision=precise
    )
    scale = 1.0 / float(grid_size * grid_size * grid_size)
    live_mask = jnp.arange(line_cos.shape[0], dtype=jnp.int32)[None, :] < lengths[:, None]
    return jnp.stack(
        [jnp.where(live_mask, out_real * scale, 0.0), jnp.where(live_mask, out_imag * scale, 0.0)]
    )


def complex_table(dft_cos, dft_sin, sign):
    from_real = jnp.stack([dft_cos, sign * dft_sin], axis=1)
    from_imag = jnp.stack([-sign * dft_sin, dft_cos], axis=1)
    return jnp.stack([from_real, from_imag])


def apply_planes(received, columns, potential, grid_size):
    depth_count = received.shape[1]
    radius = grid_size // 4
    compact = 2 * radius + 1
    col_x = columns // grid_size
    col_y = columns % grid_size
    small_x = jnp.where(col_x <= radius, col_x, col_x - grid_size + compact)
    small_y = jnp.where(col_y <= radius, col_y, col_y - grid_size + compact)
    small_index = small_x * compact + small_y
    spread = (
        jnp.zeros((2, depth_count, compact * compact), jnp.float32)
        .at[:, :, small_index]
        .add(received)
    )
    spread = jnp.transpose(spread.reshape(2, depth_count, compact, compact), (1, 2, 0, 3))
    small_axis = jnp.arange(compact, dtype=jnp.int32)
    wave_freq = jnp.where(small_axis <= radius, small_axis, small_axis - compact + grid_size)
    wave_index = jnp.arange(grid_size, dtype=jnp.int32)
    up_cos, up_sin = phase_table(wave_freq[:, None] * wave_index[None, :], grid_size)
    down_cos, down_sin = phase_table(wave_index[:, None] * wave_freq[None, :], grid_size)
    table_plus = complex_table(up_cos, up_sin, 1.0)
    table_minus = complex_table(down_cos, down_sin, -1.0)
    spread = jnp.einsum("zacb,cadx->zxdb", spread, table_plus, precision=precise)
    spread = jnp.einsum("zxcb,cbdk->zxdk", spread, table_plus, precision=precise)
    spread = spread * potential[:, :, None, :]
    spread = jnp.einsum("zxcy,cydk->zxdk", spread, table_minus, precision=precise)
    spread = jnp.einsum("zxcb,cxda->zadb", spread, table_minus, precision=precise)
    planes_flat = jnp.transpose(spread, (2, 0, 1, 3)).reshape(2, depth_count, compact * compact)
    return planes_flat[:, :, small_index]


def on_device(coefficients, potential, stick_column, stick_length, plane_start):
    plane_count = lax.axis_size("plane")
    band_count = lax.axis_size("band")
    sub_count = lax.axis_size("sub")
    owners_count = plane_count * sub_count
    plane_depth = potential.shape[0]
    grid_size = potential.shape[1]
    coef_slots = coefficients.shape[3]
    dev_slots = coefficients.shape[2]
    group_slots = band_count * dev_slots
    plane_pos = lax.axis_index("plane")
    sub_pos = lax.axis_index("sub")
    my_owner = plane_pos * sub_count + sub_pos
    plane_counts = plane_start[1:] - plane_start[:-1]
    depth_index = jnp.arange(plane_depth, dtype=jnp.int32)
    valid_plane = (depth_index[None, :] < plane_counts[:, None]).reshape(-1)
    plane_z = jnp.where(
        valid_plane, (plane_start[:-1][:, None] + depth_index[None, :]).reshape(-1), 0
    )
    line_index = jnp.arange(coef_slots, dtype=jnp.int32)
    line_cos, line_sin = phase_table(line_index[:, None] * plane_z[None, :], grid_size)
    valid_float = valid_plane.astype(jnp.float32)[None, :]
    line_cos = line_cos * valid_float
    line_sin = line_sin * valid_float
    owner_axis = jnp.arange(owners_count, dtype=jnp.int32)
    band_axis = jnp.arange(band_count, dtype=jnp.int32)
    within_axis = jnp.arange(dev_slots, dtype=jnp.int32)
    owner_major = global_slot(
        owner_axis[:, None, None],
        band_axis[None, :, None],
        within_axis[None, None, :],
        band_count,
        sub_count,
        dev_slots,
    ).reshape(-1)
    total_slots = owner_major.shape[0]
    question = plane_depth * owners_count
    group_ids = global_slot(
        my_owner, band_axis[:, None], within_axis[None, :], band_count, sub_count, dev_slots
    ).reshape(-1)
    group_len = stick_length[group_ids]
    regrouped = lax.all_to_all(coefficients, "band", split_axis=1, concat_axis=2, tiled=True)
    columns_z = inverse_columns(regrouped, group_len, line_cos, line_sin, plane_z, grid_size)
    columns_z = columns_z.reshape(2, 1, owners_count, plane_depth, group_slots)
    arrived = lax.all_to_all(columns_z, ("plane", "sub"), split_axis=2, concat_axis=4, tiled=True)
    planes_out = apply_planes(
        arrived.reshape(2, plane_depth, total_slots),
        stick_column[owner_major],
        potential,
        grid_size,
    )
    returned = lax.all_to_all(
        planes_out.reshape(2, 1, 1, plane_depth, total_slots),
        ("plane", "sub"),
        split_axis=4,
        concat_axis=2,
        tiled=True,
    )
    coef_back = forward_columns(
        returned.reshape(2, 1, question, group_slots),
        group_len,
        line_cos,
        line_sin,
        plane_z,
        grid_size,
    )
    applied = lax.all_to_all(coef_back, "band", split_axis=2, concat_axis=1, tiled=True)
    return applied


def on_device_any(coefficients, potential, stick_column, stick_length, plane_start):
    small = (
        stick_column.shape[0] <= 512 and potential.shape[0] <= HALF and coefficients.shape[2] == 8
    )
    chosen = on_device_fused if small else on_device
    return chosen(coefficients, potential, stick_column, stick_length, plane_start)


def solution(mesh):
    placed = (
        P(None, None, ("parts", "plane", "band", "sub"), None),
        P(("parts", "plane", "sub"), None, None),
        P(),
        P(),
        P(),
    )
    return jax.shard_map(
        on_device_any,
        mesh=mesh,
        in_specs=placed,
        out_specs=P(None, None, ("parts", "plane", "band", "sub"), None),
        check_vma=False,
    )
```

```python
import functools
import math

import jax
import jax.numpy as jnp
from jax import lax
from jax.experimental import pallas as pl
from jax.experimental.pallas import tpu as pltpu
from jax.sharding import PartitionSpec as P

LANES = 128
HALF = LANES // 2
SIN_TERMS = [(-1.0) ** k / math.factorial(2 * k + 1) for k in range(7)]
COS_TERMS = [(-1.0) ** k / math.factorial(2 * k) for k in range(8)]


def series(square, terms):
    total = jnp.full_like(square, terms[-1])
    for term in reversed(terms[:-1]):
        total = total * square + term
    return total


def phases(product, grid_size):
    turns = product * (1.0 / grid_size)
    rest = product - grid_size * jnp.floor(turns + 0.5)
    angle = rest * (math.pi / grid_size)
    square = angle * angle
    half_sin = angle * series(square, SIN_TERMS)
    half_cos = series(square, COS_TERMS)
    return 1.0 - 2.0 * half_sin * half_sin, 2.0 * half_sin * half_cos


def split(values):
    high = values.astype(jnp.bfloat16)
    low = (values - high.astype(jnp.float32)).astype(jnp.bfloat16)
    return high, low


def dot(left, right):
    return jnp.dot(left, right, preferred_element_type=jnp.float32)


def dot_rows(left, right):
    return lax.dot_general(
        left, right, (((1,), (1,)), ((), ())), preferred_element_type=jnp.float32
    )


def rows_of(shape):
    return lax.broadcasted_iota(jnp.int32, shape, 0)


def lanes_of(shape):
    return lax.broadcasted_iota(jnp.int32, shape, 1)


def whole(values, divisor):
    return jnp.floor((values + 0.5) * (1.0 / divisor))


def fused_kernel(
    sizes,
    start_hbm,
    length_hbm,
    column_row_hbm,
    length_row_hbm,
    coef_hbm,
    pot_hbm,
    out_ref,
    start_smem,
    length_smem,
    column_row,
    length_row,
    coef_ref,
    line_high,
    line_low,
    send_buf,
    recv_buf,
    ret_buf,
    back_buf,
    pot_vmem,
    combined,
    x_cos,
    x_sin,
    y_up,
    y_down,
    values,
    result,
    pot_sem,
    small_sem,
    out_sems,
    home_sems,
):
    plane_count, band_count, sub_count, owners, depth, grid, slots, dev_slots, coef_slots, block = sizes
    span = -(-depth // 16) * 16
    devices = plane_count * band_count * sub_count
    half_grid = grid // 2
    wide = y_down.shape[0] // 2

    part = lax.axis_index("parts")
    plane_pos = lax.axis_index("plane")
    band_pos = lax.axis_index("band")
    sub_pos = lax.axis_index("sub")
    me = (plane_pos * band_count + band_pos) * sub_count + sub_pos
    my_owner = plane_pos * sub_count + sub_pos

    def wrap(position, offset, count):
        moved = position + offset
        return jnp.where(moved >= count, moved - count, moved)

    def place(step):
        other_plane = wrap(plane_pos, step[0], plane_count)
        other_band = wrap(band_pos, step[1], band_count)
        other_sub = wrap(sub_pos, step[2], sub_count)
        owner = other_plane * sub_count + other_sub
        other = (other_plane * band_count + other_band) * sub_count + other_sub
        tile = owner * band_count + other_band
        return other, tile, (part, other_plane, other_band, other_sub)

    steps = [
        (p, b, s)
        for p in sorted(range(plane_count), key=lambda p: -min(p, plane_count - p))
        for b in reversed(range(band_count))
        for s in reversed(range(sub_count))
        if p + b + s > 0
    ]
    places = [place(step) for step in steps]
    my_tile = my_owner * band_count + band_pos

    small_copies = [
        pltpu.make_async_copy(source, target, small_sem.at[i])
        for i, (source, target) in enumerate(
            [
                (start_hbm, start_smem),
                (length_hbm, length_smem),
                (coef_hbm, coef_ref),
                (column_row_hbm, column_row),
                (length_row_hbm, length_row),
            ]
        )
    ]
    for copy in small_copies:
        copy.start()
    barrier = pltpu.get_barrier_semaphore()
    for _, _, device in places:
        pl.semaphore_signal(
            barrier, inc=1, device_id=device, device_id_type=pl.DeviceIdType.MESH
        )
    pot_copy = pltpu.make_async_copy(pot_hbm, pot_vmem, pot_sem)
    pot_copy.start()

    for copy in small_copies:
        copy.wait()

    def line_block(owner, carry):
        first = start_smem[owner]
        count = start_smem[owner + 1] - first
        shape = (span, coef_slots)
        row = rows_of(shape)
        product = (row + first).astype(jnp.float32) * lanes_of(shape).astype(jnp.float32)
        cos, sin = phases(product, float(grid))
        held = row < count
        cos = jnp.where(held, cos, 0.0)
        sin = jnp.where(held, sin, 0.0)
        blank = jnp.zeros((HALF - span, 2 * coef_slots), jnp.float32)
        rows = jnp.concatenate(
            [
                jnp.concatenate([cos, -sin], axis=1),
                blank,
                jnp.concatenate([sin, cos], axis=1),
                blank,
            ],
            axis=0,
        )
        high, low = split(rows)
        at = pl.ds(pl.multiple_of(owner * LANES, LANES), LANES)
        line_high[at, :] = high
        line_low[at, :] = low
        return carry

    lax.fori_loop(0, owners, line_block, 0, unroll=True)

    lane_small = lanes_of((dev_slots, coef_slots))
    row_small = rows_of((dev_slots, coef_slots))
    own_length = jnp.zeros((dev_slots, coef_slots), jnp.int32)
    for slot in range(dev_slots):
        own_length = jnp.where(row_small == slot, length_smem[me * dev_slots + slot], own_length)
    live = lane_small < own_length
    held = jnp.concatenate(
        [
            jnp.concatenate(
                [jnp.where(live, coef_ref[0, b], 0.0), jnp.where(live, coef_ref[1, b], 0.0)], axis=1
            )
            for b in range(band_count)
        ],
        axis=0,
    )
    high, low = split(held)
    both = dot_rows(jnp.concatenate([high, low], axis=0), line_high[...])
    rows = band_count * dev_slots
    sent = both[:rows] + both[rows:] + dot_rows(high, line_low[...])
    for owner in range(owners):
        for b in range(band_count):
            send_buf[owner * band_count + b] = sent[
                b * dev_slots : (b + 1) * dev_slots, owner * LANES : (owner + 1) * LANES
            ]

    column = column_row[...].astype(jnp.float32)
    column_x = whole(column, grid)
    column_y = column - grid * column_x
    cos, sin = phases(rows_of((grid, slots)).astype(jnp.float32) * column_x, float(grid))
    x_cos[...] = cos
    x_sin[...] = sin
    cos, sin = phases(rows_of((wide, slots)).astype(jnp.float32) * column_y, float(grid))
    high, low = split(jnp.concatenate([cos, sin], axis=0))
    y_down[:, :slots] = high
    y_down[:, slots:] = low
    high, low = split(jnp.concatenate([cos.T, sin.T], axis=1))
    y_up[:slots] = high
    y_up[slots : 2 * slots] = high
    y_up[2 * slots :] = low
    half_length = whole(length_row[...].astype(jnp.float32), 2)
    my_first = start_smem[my_owner]
    turn_cos, turn_sin = phases(
        (rows_of((span, slots)) + my_first).astype(jnp.float32) * half_length, float(grid)
    )

    pl.semaphore_wait(barrier, devices - 1)

    def send(source, target, sems, device):
        return pltpu.make_async_remote_copy(
            src_ref=source,
            dst_ref=target,
            send_sem=sems.at[0],
            recv_sem=sems.at[1],
            device_id=device,
            device_id_type=pl.DeviceIdType.MESH,
        )

    def all_of(buffer, sems):
        others = buffer.at[pl.ds(0, devices - 1)]
        return send(others, others, sems, places[0][2])

    for _, tile, device in places:
        send(send_buf.at[tile], recv_buf.at[me], out_sems, device).start()
    recv_buf[me] = send_buf[my_tile]

    row = rows_of((grid, wide))
    lane = lanes_of((grid, wide))
    same = jnp.where((row == lane) & (lane <= half_grid), 1.0, 0.0)
    mirror = jnp.where((row + lane == grid) & (lane < half_grid), 1.0, 0.0)
    inner = jnp.where((row == lane) & (lane < half_grid) & (lane > 0), 1.0, 0.0)
    pairing = jnp.concatenate([same + mirror, inner - mirror], axis=1).astype(jnp.bfloat16)
    pot_copy.wait()

    def combine(step, carry):
        for i in range(block):
            z = step * block + i
            high, low = split(pot_vmem[z])
            combined[z] = dot(high, pairing) + dot(low, pairing)
        return carry

    lax.fori_loop(0, depth // block, combine, 0)
    result[...] = jnp.zeros_like(result)

    all_of(recv_buf, out_sems).wait_recv()
    turned = recv_buf[...].reshape(slots, LANES).T
    got_real = turned[:span]
    got_imag = turned[HALF : HALF + span]
    values[0] = got_real * turn_cos + got_imag * turn_sin
    values[1] = got_imag * turn_cos - got_real * turn_sin

    def planes(step, carry):
        for i in range(depth):
            z = i
            real = values[0, pl.ds(z, 1), :]
            imag = values[1, pl.ds(z, 1), :]
            ax = x_cos[...]
            bx = x_sin[...]
            high, low = split(
                jnp.concatenate([ax * real - bx * imag, ax * imag + bx * real], axis=0)
            )
            psi = dot(jnp.concatenate([high, low, high], axis=1), y_up[...])
            even_real, odd_real = psi[:grid, :wide], psi[:grid, wide:]
            even_imag, odd_imag = psi[grid:, :wide], psi[grid:, wide:]
            even = combined[z, :, :wide]
            odd = combined[z, :, wide:]
            product = jnp.concatenate(
                [
                    jnp.concatenate(
                        [
                            even * even_real - odd * odd_imag,
                            odd * even_imag + even * odd_real,
                        ],
                        axis=1,
                    ),
                    jnp.concatenate(
                        [
                            even * even_imag + odd * odd_real,
                            even * odd_imag - odd * even_real,
                        ],
                        axis=1,
                    ),
                ],
                axis=0,
            )
            high, low = split(product)
            first = dot(high, y_down[...])
            back = first[:, :slots] + first[:, slots:] + dot(low, y_down[:, :slots])
            back_real, back_imag = back[:grid], back[grid:]
            result[pl.ds(z, 1), :] = jnp.sum(ax * back_real + bx * back_imag, axis=0, keepdims=True)
            result[pl.ds(HALF + z, 1), :] = jnp.sum(
                ax * back_imag - bx * back_real, axis=0, keepdims=True
            )
        return carry

    planes(0, 0)

    out_real = result[:span]
    out_imag = result[HALF : HALF + span]
    blank = jnp.zeros((HALF - span, slots), jnp.float32)
    ret_buf[...] = jnp.concatenate(
        [
            out_real * turn_cos - out_imag * turn_sin,
            blank,
            out_imag * turn_cos + out_real * turn_sin,
            blank,
        ],
        axis=0,
    ).T.reshape(devices, dev_slots, LANES)
    for other, _, device in places:
        send(ret_buf.at[other], back_buf.at[my_tile], home_sems, device).start()
    back_buf[my_tile] = ret_buf[me]
    all_of(back_buf, home_sems).wait_recv()

    lines = jnp.concatenate(
        [
            jnp.concatenate([back_buf[owner * band_count + b] for b in range(band_count)], axis=0)
            for owner in range(owners)
        ],
        axis=1,
    )
    high, low = split(lines)
    both = dot(jnp.concatenate([high, low], axis=0), line_high[...])
    applied = both[:rows] + both[rows:] + dot(high, line_low[...])
    applied = applied * (1.0 / float(grid * grid * grid))
    for b in range(band_count):
        for c in range(2):
            piece = applied[
                b * dev_slots : (b + 1) * dev_slots, c * coef_slots : (c + 1) * coef_slots
            ]
            out_ref[c, b] = jnp.where(live, piece, 0.0)

    all_of(send_buf, out_sems).wait_send()
    all_of(ret_buf, home_sems).wait_send()


def on_device_fused(coefficients, potential, stick_column, stick_length, plane_start):
    plane_count = lax.axis_size("plane")
    band_count = lax.axis_size("band")
    sub_count = lax.axis_size("sub")
    owners = plane_count * sub_count
    depth, grid = potential.shape[0], potential.shape[1]
    dev_slots, coef_slots = coefficients.shape[2], coefficients.shape[3]
    slots = stick_column.shape[0]
    devices = plane_count * band_count * sub_count
    wide = -(-(grid // 2 + 1) // LANES) * LANES
    span = -(-depth // 16) * 16
    block = max(k for k in range(1, 6) if depth % k == 0)
    sizes = (
        plane_count, band_count, sub_count, owners, depth, grid, slots, dev_slots, coef_slots, block
    )
    f32, bf16 = jnp.float32, jnp.bfloat16
    vmem = pl.BlockSpec(memory_space=pltpu.VMEM)
    return pl.pallas_call(
        functools.partial(fused_kernel, sizes),
        out_shape=jax.ShapeDtypeStruct(coefficients.shape, f32),
        in_specs=[pl.BlockSpec(memory_space=pltpu.HBM)] * 6,
        out_specs=vmem,
        scratch_shapes=[
            pltpu.SMEM(plane_start.shape, jnp.int32),
            pltpu.SMEM(stick_length.shape, jnp.int32),
            pltpu.VMEM((1, slots), jnp.int32),
            pltpu.VMEM((1, slots), jnp.int32),
            pltpu.VMEM(coefficients.shape, f32),
            pltpu.VMEM((owners * LANES, 2 * coef_slots), bf16),
            pltpu.VMEM((owners * LANES, 2 * coef_slots), bf16),
            pltpu.VMEM((devices, dev_slots, LANES), f32),
            pltpu.VMEM((devices, dev_slots, LANES), f32),
            pltpu.VMEM((devices, dev_slots, LANES), f32),
            pltpu.VMEM((devices, dev_slots, LANES), f32),
            pltpu.VMEM(potential.shape, f32),
            pltpu.VMEM((depth, grid, 2 * wide), f32),
            pltpu.VMEM((grid, slots), f32),
            pltpu.VMEM((grid, slots), f32),
            pltpu.VMEM((3 * slots, 2 * wide), bf16),
            pltpu.VMEM((2 * wide, 2 * slots), bf16),
            pltpu.VMEM((2, span, slots), f32),
            pltpu.VMEM((LANES, slots), f32),
            pltpu.SemaphoreType.DMA,
            pltpu.SemaphoreType.DMA((5,)),
            pltpu.SemaphoreType.DMA((2,)),
            pltpu.SemaphoreType.DMA((2,)),
        ],
        compiler_params=pltpu.CompilerParams(
            collective_id=0, has_side_effects=True, vmem_limit_bytes=64 * 1024 * 1024
        ),
        cost_estimate=pl.CostEstimate(
            flops=4 * depth * 2 * grid * slots * 2 * wide,
            bytes_accessed=potential.size * 4,
            transcendentals=0,
        ),
    )(
        plane_start,
        stick_length,
        stick_column.reshape(1, slots),
        stick_length.reshape(1, slots),
        coefficients,
        potential,
    )


two_pi = 2.0 * math.pi
precise = lax.Precision.HIGHEST


def phase_table(product, grid_size):
    angle = (product % grid_size).astype(jnp.float32) * (two_pi / grid_size)
    return (jnp.cos(angle), jnp.sin(angle))


def global_slot(owner_src, band_src, within, band_count, sub_count, dev_slots):
    return (
        (owner_src // sub_count * band_count + band_src) * sub_count + owner_src % sub_count
    ) * dev_slots + within


def inverse_columns(parts, lengths, line_cos, line_sin, plane_z, grid_size):
    live_mask = jnp.arange(parts.shape[3], dtype=jnp.int32)[None, :] < lengths[:, None]
    real_part = jnp.where(live_mask, parts[0], 0.0)
    imag_part = jnp.where(live_mask, parts[1], 0.0)
    first_real = jnp.einsum("bsl,lq->bqs", real_part, line_cos, precision=precise) - jnp.einsum(
        "bsl,lq->bqs", imag_part, line_sin, precision=precise
    )
    first_imag = jnp.einsum("bsl,lq->bqs", real_part, line_sin, precision=precise) + jnp.einsum(
        "bsl,lq->bqs", imag_part, line_cos, precision=precise
    )
    shift_cos, shift_sin = phase_table(plane_z[:, None] * (lengths // 2)[None, :], grid_size)
    out_real = first_real * shift_cos + first_imag * shift_sin
    out_imag = first_imag * shift_cos - first_real * shift_sin
    return jnp.stack([out_real, out_imag])


def forward_columns(data, lengths, line_cos, line_sin, plane_z, grid_size):
    shift_cos, shift_sin = phase_table(plane_z[:, None] * (lengths // 2)[None, :], grid_size)
    turn_real = data[0] * shift_cos - data[1] * shift_sin
    turn_imag = data[1] * shift_cos + data[0] * shift_sin
    out_real = jnp.einsum("bqs,lq->bsl", turn_real, line_cos, precision=precise) + jnp.einsum(
        "bqs,lq->bsl", turn_imag, line_sin, precision=precise
    )
    out_imag = jnp.einsum("bqs,lq->bsl", turn_imag, line_cos, precision=precise) - jnp.einsum(
        "bqs,lq->bsl", turn_real, line_sin, precision=precise
    )
    scale = 1.0 / float(grid_size * grid_size * grid_size)
    live_mask = jnp.arange(line_cos.shape[0], dtype=jnp.int32)[None, :] < lengths[:, None]
    return jnp.stack(
        [jnp.where(live_mask, out_real * scale, 0.0), jnp.where(live_mask, out_imag * scale, 0.0)]
    )


def complex_table(dft_cos, dft_sin, sign):
    from_real = jnp.stack([dft_cos, sign * dft_sin], axis=1)
    from_imag = jnp.stack([-sign * dft_sin, dft_cos], axis=1)
    return jnp.stack([from_real, from_imag])


def apply_planes(received, columns, potential, grid_size):
    depth_count = received.shape[1]
    radius = grid_size // 4
    compact = 2 * radius + 1
    col_x = columns // grid_size
    col_y = columns % grid_size
    small_x = jnp.where(col_x <= radius, col_x, col_x - grid_size + compact)
    small_y = jnp.where(col_y <= radius, col_y, col_y - grid_size + compact)
    small_index = small_x * compact + small_y
    spread = (
        jnp.zeros((2, depth_count, compact * compact), jnp.float32)
        .at[:, :, small_index]
        .add(received)
    )
    spread = jnp.transpose(spread.reshape(2, depth_count, compact, compact), (1, 2, 0, 3))
    small_axis = jnp.arange(compact, dtype=jnp.int32)
    wave_freq = jnp.where(small_axis <= radius, small_axis, small_axis - compact + grid_size)
    wave_index = jnp.arange(grid_size, dtype=jnp.int32)
    up_cos, up_sin = phase_table(wave_freq[:, None] * wave_index[None, :], grid_size)
    down_cos, down_sin = phase_table(wave_index[:, None] * wave_freq[None, :], grid_size)
    table_plus = complex_table(up_cos, up_sin, 1.0)
    table_minus = complex_table(down_cos, down_sin, -1.0)
    spread = jnp.einsum("zacb,cadx->zxdb", spread, table_plus, precision=precise)
    spread = jnp.einsum("zxcb,cbdk->zxdk", spread, table_plus, precision=precise)
    spread = spread * potential[:, :, None, :]
    spread = jnp.einsum("zxcy,cydk->zxdk", spread, table_minus, precision=precise)
    spread = jnp.einsum("zxcb,cxda->zadb", spread, table_minus, precision=precise)
    planes_flat = jnp.transpose(spread, (2, 0, 1, 3)).reshape(2, depth_count, compact * compact)
    return planes_flat[:, :, small_index]


def on_device(coefficients, potential, stick_column, stick_length, plane_start):
    plane_count = lax.axis_size("plane")
    band_count = lax.axis_size("band")
    sub_count = lax.axis_size("sub")
    owners_count = plane_count * sub_count
    plane_depth = potential.shape[0]
    grid_size = potential.shape[1]
    coef_slots = coefficients.shape[3]
    dev_slots = coefficients.shape[2]
    group_slots = band_count * dev_slots
    plane_pos = lax.axis_index("plane")
    sub_pos = lax.axis_index("sub")
    my_owner = plane_pos * sub_count + sub_pos
    plane_counts = plane_start[1:] - plane_start[:-1]
    depth_index = jnp.arange(plane_depth, dtype=jnp.int32)
    valid_plane = (depth_index[None, :] < plane_counts[:, None]).reshape(-1)
    plane_z = jnp.where(
        valid_plane, (plane_start[:-1][:, None] + depth_index[None, :]).reshape(-1), 0
    )
    line_index = jnp.arange(coef_slots, dtype=jnp.int32)
    line_cos, line_sin = phase_table(line_index[:, None] * plane_z[None, :], grid_size)
    valid_float = valid_plane.astype(jnp.float32)[None, :]
    line_cos = line_cos * valid_float
    line_sin = line_sin * valid_float
    owner_axis = jnp.arange(owners_count, dtype=jnp.int32)
    band_axis = jnp.arange(band_count, dtype=jnp.int32)
    within_axis = jnp.arange(dev_slots, dtype=jnp.int32)
    owner_major = global_slot(
        owner_axis[:, None, None],
        band_axis[None, :, None],
        within_axis[None, None, :],
        band_count,
        sub_count,
        dev_slots,
    ).reshape(-1)
    total_slots = owner_major.shape[0]
    question = plane_depth * owners_count
    group_ids = global_slot(
        my_owner, band_axis[:, None], within_axis[None, :], band_count, sub_count, dev_slots
    ).reshape(-1)
    group_len = stick_length[group_ids]
    regrouped = lax.all_to_all(coefficients, "band", split_axis=1, concat_axis=2, tiled=True)
    columns_z = inverse_columns(regrouped, group_len, line_cos, line_sin, plane_z, grid_size)
    columns_z = columns_z.reshape(2, 1, owners_count, plane_depth, group_slots)
    arrived = lax.all_to_all(columns_z, ("plane", "sub"), split_axis=2, concat_axis=4, tiled=True)
    planes_out = apply_planes(
        arrived.reshape(2, plane_depth, total_slots),
        stick_column[owner_major],
        potential,
        grid_size,
    )
    returned = lax.all_to_all(
        planes_out.reshape(2, 1, 1, plane_depth, total_slots),
        ("plane", "sub"),
        split_axis=4,
        concat_axis=2,
        tiled=True,
    )
    coef_back = forward_columns(
        returned.reshape(2, 1, question, group_slots),
        group_len,
        line_cos,
        line_sin,
        plane_z,
        grid_size,
    )
    applied = lax.all_to_all(coef_back, "band", split_axis=2, concat_axis=1, tiled=True)
    return applied


def on_device_any(coefficients, potential, stick_column, stick_length, plane_start):
    small = (
        stick_column.shape[0] <= 512 and potential.shape[0] <= HALF and coefficients.shape[2] == 8
    )
    chosen = on_device_fused if small else on_device
    return chosen(coefficients, potential, stick_column, stick_length, plane_start)


def solution(mesh):
    placed = (
        P(None, None, ("parts", "plane", "band", "sub"), None),
        P(("parts", "plane", "sub"), None, None),
        P(),
        P(),
        P(),
    )
    return jax.shard_map(
        on_device_any,
        mesh=mesh,
        in_specs=placed,
        out_specs=P(None, None, ("parts", "plane", "band", "sub"), None),
        check_vma=False,
    )
```
